32 devices in a mesh: tok: 8 (over y, x, core), tp: 4 (over z).
Axes of the slice: x: 2, y: 2, z: 4, core: 2. Of those that a mesh axis runs over, the one named last changes fastest.
Arguments:
- tokens: bfloat16 [8192, 1024], P('tok', 'tp'), may hold values from -6 to 6
- mix_weights: bfloat16 [10, 2, 2, 128, 128], replicated, may hold values from -0.375 to 0.375
- proj_weight: bfloat16 [1024, 2048], P('tp'), may hold values from -0.1875 to 0.1875
- pool_map: int32 [8192], P('tok'), may hold values from 0 to 1023, as said below
- out_cot: bfloat16 [1024, 2048], P('tok', 'tp'), may hold values from -6 to 6
Outputs:
- projected: bfloat16 [1024, 2048], P('tok', 'tp')
- token_grad: bfloat16 [8192, 1024], P('tok', 'tp')
- proj_grad: float32 [2048, 1024], P('tok', 'tp')
The draws below stay inside these ranges and needn't reach their ends.
Inputs may be any that keep to these rules, and one draw needn't show every extreme that they name: `pool_map`: token t names one of the 128 pooled tokens of its own block of 1024 tokens, numbers (t // 1024) * 128 onward; every pooled token is named by at least one token.
All inputs are finite; a program needn't handle non-finite values.
Results may differ from the reference program's by a relative error of at most 0.017.
Values may be sent and summed in bfloat16 or wider, within the bound.
No kernel may reach another device: no remote copies, remote signals or barrier semaphores. Data moves between devices by JAX's collectives and lax.ppermute only.
A program may use at most 64 MiB of HBM per device.

```python
import math
import jax
import jax.numpy as jnp
from jax import lax

D = 1024
E = 2048
BLK = 128
SECTIONS = 10
TOK_DEV = 1024
POOL_DEV = 128
TOKENS = 8192
POOLED = 1024


def draw_pool_map(key, part):
    blocks = TOKENS // TOK_DEV
    rank_keys = jax.random.split(jax.random.fold_in(key, 11), blocks)
    ranks = jax.vmap(lambda sub_key: jax.random.permutation(sub_key, TOK_DEV))(rank_keys)
    extra_ids = jax.random.randint(jax.random.fold_in(key, 12), (blocks, TOK_DEV), 0, POOL_DEV)
    local_ids = jnp.where(ranks < POOL_DEV, ranks, extra_ids)
    offsets = jnp.arange(blocks, dtype=jnp.int32)[:, None] * POOL_DEV
    return (local_ids + offsets).astype(jnp.int32).reshape(TOKENS)


def with_spikes(drawn, key, source, target, parts, factor):
    owner, partner = [(jnp.arange(drawn.shape[dim]) // (drawn.shape[dim] // parts)).reshape([-1 if axis == dim else 1 for axis in range(drawn.ndim)]) for dim in (source, target)]
    chosen = jax.random.permutation(key, parts)[partner]
    strong = (owner == chosen) | (owner == (partner + parts // 2) % parts)
    return jnp.where(strong, factor * drawn, drawn)


def shard_levels(key, extent, cuts, least, high):
    def one(dim, shards_of):
        draws = jax.random.uniform(jax.random.fold_in(jax.random.fold_in(key, 6), dim), (shards_of,), jnp.float32, least / len(cuts), high / len(cuts))
        return jnp.repeat(jnp.exp(draws), extent[dim] // shards_of).reshape((-1,) + (1,) * (len(extent) - dim - 1))

    factor_of = one(*cuts[0])
    for cut in cuts[1:]:
        factor_of = factor_of * one(*cut)
    return factor_of


def centred(rng, shape, deviation, reach, shards=(), kind=jnp.bfloat16):
    result = jax.random.normal(rng, shape, jnp.float32) * deviation
    if len(shards) > 0:
        result = shard_levels(rng, shape, shards, -0.22, 0.18) * result
    return jnp.clip(result, min=-reach, max=reach).astype(kind)


def heavy_noise(rng, dims, scale, reach, cuts, heavy, kind=jnp.bfloat16):
    array = scale * jax.random.normal(rng, dims, jnp.float32)
    if cuts:
        array = array * shard_levels(rng, dims, cuts, -0.22, 0.18)
    return jnp.clip(with_spikes(array, jax.random.fold_in(rng, 3), *heavy), -reach, reach).astype(kind)


def setup_inputs(seed: int = 0) -> dict:
    arg_keys = jax.random.split(jax.random.key(seed), 6)
    return {
        "tokens": centred(arg_keys[0], (TOKENS, D), 1.0, 6.0, ((0, 8), (1, 4))),
        "mix_weights": centred(arg_keys[1], (SECTIONS, 2, 2, BLK, BLK), (2 * BLK) ** -0.5, 0.375),
        "proj_weight": centred(arg_keys[2], (D, E), D ** -0.5, 0.1875, ((0, 4),)),
        "pool_map": draw_pool_map(jax.random.fold_in(arg_keys[5], 71), 0),
        "out_cot": heavy_noise(arg_keys[4], (POOLED, E), 1.0, 6.0, ((0, 8), (1, 4)), (0, 1, 8, 2.0)),
    }


def contract(matrix, operand, backward):
    pattern = 'ji,...jf->...if' if backward else 'ij,...jf->...if'
    return jnp.einsum(pattern, matrix.astype(jnp.float32), operand.astype(jnp.float32))

def apply_section(source, section_mats, bit_index, backward):
    full_shape = source.shape
    nblocks = full_shape[0]
    paired = source.reshape((nblocks >> bit_index + 1, 2, 1 << bit_index) + full_shape[1:])
    lower_half = paired[:, 0]
    upper_half = paired[:, 1]
    if backward:
        new_lower = contract(section_mats[0, 0], lower_half, True) + contract(section_mats[1, 0], upper_half, True)
        new_upper = contract(section_mats[0, 1], lower_half, True) + contract(section_mats[1, 1], upper_half, True)
    else:
        new_lower = contract(section_mats[0, 0], lower_half, False) + contract(section_mats[0, 1], upper_half, False)
        new_upper = contract(section_mats[1, 0], lower_half, False) + contract(section_mats[1, 1], upper_half, False)
    joined = jnp.stack([new_lower.astype(jnp.bfloat16), new_upper.astype(jnp.bfloat16)], axis=1)
    return joined.reshape(full_shape)

def reference(tokens, mix_weights, proj_weight, pool_map, out_cot):
    token_count = tokens.shape[0]
    feat_width = tokens.shape[1]
    block_rows = mix_weights.shape[-1]
    section_count = mix_weights.shape[0]
    block_count = token_count // block_rows
    all_bits = block_count.bit_length() - 1
    section_bits = [section_id % all_bits for section_id in range(section_count)]

    def mix_tokens(source, backward):
        groups = source.reshape(token_count, feat_width // 128, 128).transpose(1, 0, 2)

        def mix_slab(slab):
            field_now = slab.reshape(block_count, block_rows, 128)
            section_order = list(range(section_count))
            if backward:
                section_order = section_order[::-1]
            for section_id in section_order:
                field_now = apply_section(field_now, mix_weights[section_id], section_bits[section_id], backward)
            return field_now.reshape(token_count, 128)
        mixed_groups = lax.map(mix_slab, groups)
        return mixed_groups.transpose(1, 0, 2).reshape(token_count, feat_width)
    mixed = mix_tokens(tokens, False)
    pooled_rows = out_cot.shape[0]
    group_sums = jax.ops.segment_sum(mixed.astype(jnp.float32), pool_map, num_segments=pooled_rows)
    counts = jax.ops.segment_sum(jnp.ones((token_count,), jnp.float32), pool_map, num_segments=pooled_rows)
    pooled = (group_sums / counts[:, None]).astype(jnp.bfloat16)
    projected = jnp.dot(pooled, proj_weight, preferred_element_type=jnp.float32).astype(jnp.bfloat16)
    d_pooled = jnp.dot(out_cot, proj_weight.T, preferred_element_type=jnp.float32)
    back_rows = jnp.take(d_pooled / counts[:, None], pool_map, axis=0).astype(jnp.bfloat16)
    token_grad = mix_tokens(back_rows, True)
    grad_scale = 1.0 / math.sqrt(pooled_rows)
    proj_grad = jnp.dot(out_cot.T, pooled, preferred_element_type=jnp.float32) * grad_scale
    return (projected, token_grad, proj_grad)
```

```python
import functools
import math

import jax
import jax.numpy as jnp
from jax import lax
from jax.experimental import pallas as pl
from jax.experimental.pallas import tpu as pltpu
from jax.sharding import PartitionSpec as P

F32 = jnp.float32
BF16 = jnp.bfloat16
VMEM_LIMIT = 40 * 1024 * 1024
NT = (((1,), (1,)), ((), ()))
NN = (((1,), (0,)), ((), ()))


def contract(matrix, operand, backward):
    pattern = "ji,...j->...i" if backward else "ij,...j->...i"
    return jnp.einsum(pattern, matrix, operand, preferred_element_type=F32)


def plain_section(field_now, section_mats, bit_index, backward):
    full_shape = field_now.shape
    paired = field_now.reshape(
        (full_shape[0], full_shape[1] >> bit_index + 1, 2, 1 << bit_index, full_shape[2])
    )
    lower, upper = paired[:, :, 0], paired[:, :, 1]
    halves = []
    for h in range(2):
        pair = (section_mats[0, h], section_mats[1, h]) if backward else section_mats[h]
        halves.append(contract(pair[0], lower, backward) + contract(pair[1], upper, backward))
    joined = jnp.stack([half.astype(BF16) for half in halves], axis=2)
    return joined.reshape(full_shape)


def plain_mix(field, mix_weights, section_bits, backward):
    owners, feats, toks = field.shape
    block_rows = mix_weights.shape[-1]
    now = field.transpose(1, 0, 2).reshape(feats, owners * toks // block_rows, block_rows)
    order = list(enumerate(section_bits))
    for section_id, bit in order[::-1] if backward else order:
        now = plain_section(now, mix_weights[section_id], bit, backward)
    return now.reshape(feats, owners, toks).transpose(1, 0, 2)


def one_hot(map_row, pool_rows):
    ids = lax.broadcasted_iota(jnp.int32, (pool_rows, map_row.shape[-1]), 0)
    return (map_row == ids).astype(BF16)


def run_sections(field, other, mix_ref, section_bits, backward):
    blocks, feats, rows = field.shape
    order = list(enumerate(section_bits))
    for section_id, bit in order[::-1] if backward else order:
        m = [[mix_ref[section_id, a, b] for b in range(2)] for a in range(2)]
        full = jnp.concatenate(
            [jnp.concatenate(m[0], axis=1), jnp.concatenate(m[1], axis=1)], axis=0
        )
        lows = [b for b in range(blocks) if not (b >> bit) & 1]
        step = max(1, 512 // feats)
        for at in range(0, len(lows), step):
            part = lows[at : at + step]
            low = jnp.concatenate([field[b] for b in part], axis=0)
            high = jnp.concatenate([field[b + (1 << bit)] for b in part], axis=0)
            pair = jnp.concatenate([low, high], axis=1)
            out = lax.dot_general(
                pair, full, NN if backward else NT, preferred_element_type=F32
            ).astype(BF16)
            for n, b in enumerate(part):
                other[b] = out[n * feats : (n + 1) * feats, :rows]
                other[b + (1 << bit)] = out[n * feats : (n + 1) * feats, rows:]
        field, other = other, field
    return field


def forward_kernel(section_bits, pool_rows, x_ref, map_ref, mix_ref, pooled_ref, a_ref, b_ref):
    owners, feats, toks = x_ref.shape
    rows = a_ref.shape[2]
    per = toks // rows
    for g in range(owners):
        for n in range(per):
            a_ref[g * per + n] = x_ref[g, :, n * rows : (n + 1) * rows]
    done = run_sections(a_ref, b_ref, mix_ref, section_bits, False)
    ones = jnp.ones((16, toks), BF16)
    for g in range(owners):
        mine = jnp.concatenate([done[g * per + n] for n in range(per)], axis=1)
        sums = lax.dot_general(
            jnp.concatenate([mine, ones], axis=0),
            one_hot(map_ref[g : g + 1, :], pool_rows),
            NT,
            preferred_element_type=F32,
        )
        pooled_ref[:, g * pool_rows : (g + 1) * pool_rows] = (
            sums[:feats] / sums[feats : feats + 1]
        ).astype(BF16)


def backward_kernel(section_bits, pool_rows, d_ref, map_ref, mix_ref, grad_ref, a_ref, b_ref):
    owners, feats, toks = grad_ref.shape
    rows = a_ref.shape[2]
    per = toks // rows
    for g in range(owners):
        spread = lax.dot_general(
            d_ref[g], one_hot(map_ref[g : g + 1, :], pool_rows), NN, preferred_element_type=F32
        ).astype(BF16)
        for n in range(per):
            a_ref[g * per + n] = spread[:, n * rows : (n + 1) * rows]
    done = run_sections(a_ref, b_ref, mix_ref, section_bits, True)
    for g in range(owners):
        for n in range(per):
            grad_ref[g, :, n * rows : (n + 1) * rows] = done[g * per + n]


def call(kernel, operands, out_shape, scratch, flops, bytes_accessed, name):
    return pl.pallas_call(
        kernel,
        out_shape=out_shape,
        in_specs=[pl.BlockSpec(memory_space=pltpu.VMEM)] * len(operands),
        out_specs=pl.BlockSpec(memory_space=pltpu.VMEM),
        scratch_shapes=scratch,
        compiler_params=pltpu.CompilerParams(vmem_limit_bytes=VMEM_LIMIT),
        cost_estimate=pl.CostEstimate(
            flops=flops, bytes_accessed=bytes_accessed, transcendentals=0
        ),
        name=name,
    )(*operands)


def forward_mix(field, maps, mix_weights, section_bits, pool_rows):
    owners, feats, toks = field.shape
    rows = mix_weights.shape[-1]
    if feats % 16:
        mixed = plain_mix(field, mix_weights, section_bits, False)
        hot = jax.vmap(lambda m: one_hot(m[None], pool_rows))(maps)
        sums = jnp.einsum("gft,gpt->gfp", mixed, hot, preferred_element_type=F32)
        counts = jnp.sum(hot.astype(F32), axis=2)
        pooled = (sums / counts[:, None]).astype(BF16)
        return pooled.transpose(1, 0, 2).reshape(feats, owners * pool_rows)
    blocks = owners * toks // rows
    scratch = [pltpu.VMEM((blocks, feats, rows), BF16)] * 2
    return call(
        functools.partial(forward_kernel, section_bits, pool_rows),
        (field, maps, mix_weights),
        jax.ShapeDtypeStruct((feats, owners * pool_rows), BF16),
        scratch,
        len(section_bits) * 4 * rows * owners * toks * feats,
        field.size * 2 + mix_weights.size * 2,
        "forward_mix",
    )


def backward_mix(d_pooled, maps, mix_weights, section_bits):
    owners, feats, pool_rows = d_pooled.shape
    toks = maps.shape[1]
    rows = mix_weights.shape[-1]
    if feats % 16:
        hot = jax.vmap(lambda m: one_hot(m[None], pool_rows))(maps)
        spread = jnp.einsum("gfp,gpt->gft", d_pooled, hot, preferred_element_type=F32)
        return plain_mix(spread.astype(BF16), mix_weights, section_bits, True)
    blocks = owners * toks // rows
    scratch = [pltpu.VMEM((blocks, feats, rows), BF16)] * 2
    return call(
        functools.partial(backward_kernel, section_bits, pool_rows),
        (d_pooled, maps, mix_weights),
        jax.ShapeDtypeStruct((owners, feats, toks), BF16),
        scratch,
        len(section_bits) * 4 * rows * owners * toks * feats,
        owners * feats * toks * 2 + mix_weights.size * 2,
        "backward_mix",
    )


def shards(tokens, mix_weights, proj_weight, pool_map, out_cot):
    toks, feats_tp = tokens.shape
    section_count, block_rows = mix_weights.shape[0], mix_weights.shape[-1]
    owners, groups = lax.axis_size("tok"), lax.axis_size("tp")
    pool_rows, outs_tp = out_cot.shape
    feats = feats_tp // owners
    outs = outs_tp * groups
    all_bits = (owners * toks // block_rows).bit_length() - 1
    section_bits = [section_id % all_bits for section_id in range(section_count)]
    me = lax.axis_index("tok")

    local_map = pool_map - me * pool_rows
    maps = lax.all_gather(local_map, "tok", axis=0)
    field = lax.all_to_all(
        tokens.T.reshape(owners, feats, toks), "tok", split_axis=0, concat_axis=0, tiled=True
    )
    cot = lax.all_gather(out_cot, "tp", axis=1, tiled=True)
    counts = jnp.sum(one_hot(local_map[None], pool_rows).astype(F32), axis=1)

    d_pooled = lax.dot_general(proj_weight, cot, NT, preferred_element_type=F32)
    d_pooled = (d_pooled / counts[None, :]).astype(BF16).reshape(owners, feats, pool_rows)
    d_pooled = lax.all_to_all(d_pooled, "tok", split_axis=0, concat_axis=0, tiled=True)
    cot_cols = cot.reshape(pool_rows, owners, outs // owners).transpose(1, 0, 2)
    cot_cols = lax.all_to_all(cot_cols, "tok", split_axis=0, concat_axis=0, tiled=True)
    cot_cols = cot_cols.reshape(owners * pool_rows, outs // owners)

    pooled = forward_mix(field, maps, mix_weights, section_bits, pool_rows)
    pooled = lax.all_gather(pooled, "tok", axis=0, tiled=True)

    grad = backward_mix(d_pooled, maps, mix_weights, section_bits)
    grad = lax.all_to_all(grad, "tok", split_axis=0, concat_axis=0, tiled=True)
    token_grad = grad.reshape(feats_tp, toks).T

    mine = lax.dynamic_slice_in_dim(pooled, me * pool_rows, pool_rows, axis=1)
    share = lax.dot_general(
        mine, proj_weight, (((0,), (0,)), ((), ())), preferred_element_type=F32
    ).astype(BF16)
    share = share.reshape(pool_rows, groups, outs_tp).transpose(1, 0, 2)
    share = lax.all_to_all(share, "tp", split_axis=0, concat_axis=0, tiled=True)
    projected = jnp.sum(share.astype(F32), axis=0).astype(BF16)

    proj_grad = lax.dot_general(
        cot_cols, pooled, (((0,), (1,)), ((), ())), preferred_element_type=F32
    ) * (1.0 / math.sqrt(pool_rows * owners))
    return (projected, token_grad, proj_grad)


def solution(mesh):
    in_specs = (P("tok", "tp"), P(), P("tp", None), P("tok"), P("tok", "tp"))
    out_specs = (P("tok", "tp"), P("tok", "tp"), P("tok", "tp"))
    return jax.shard_map(shards, mesh=mesh, in_specs=in_specs, out_specs=out_specs, check_vma=False)
```

```python
import functools
import math

import jax
import jax.numpy as jnp
from jax import lax
from jax.experimental import pallas as pl
from jax.experimental.pallas import tpu as pltpu
from jax.sharding import PartitionSpec as P

F32 = jnp.float32
BF16 = jnp.bfloat16
VMEM_LIMIT = 40 * 1024 * 1024
NT = (((1,), (1,)), ((), ()))
NN = (((1,), (0,)), ((), ()))
TAIL = 16
LONG = 30_000_000_000


def contract(matrix, operand, backward):
    pattern = "ji,...j->...i" if backward else "ij,...j->...i"
    return jnp.einsum(pattern, matrix, operand, preferred_element_type=jnp.float32)


def local_section(field_now, section_mats, bit_index, backward, block_axis):
    full_shape = field_now.shape
    nblocks = full_shape[block_axis]
    split_shape = (
        full_shape[:block_axis]
        + (nblocks >> bit_index + 1, 2, 1 << bit_index)
        + full_shape[block_axis + 1 :]
    )
    paired = field_now.reshape(split_shape)
    lower_half = lax.index_in_dim(paired, 0, block_axis + 1, keepdims=False)
    upper_half = lax.index_in_dim(paired, 1, block_axis + 1, keepdims=False)
    if backward:
        new_lower = contract(section_mats[0, 0], lower_half, True) + contract(
            section_mats[1, 0], upper_half, True
        )
        new_upper = contract(section_mats[0, 1], lower_half, True) + contract(
            section_mats[1, 1], upper_half, True
        )
    else:
        new_lower = contract(section_mats[0, 0], lower_half, False) + contract(
            section_mats[0, 1], upper_half, False
        )
        new_upper = contract(section_mats[1, 0], lower_half, False) + contract(
            section_mats[1, 1], upper_half, False
        )
    joined = jnp.stack(
        [new_lower.astype(jnp.bfloat16), new_upper.astype(jnp.bfloat16)], axis=block_axis + 1
    )
    return joined.reshape(full_shape)


def mix_tokens(source, mix_weights, section_bits, backward):
    block_rows = mix_weights.shape[-1]
    section_order = list(range(len(section_bits)))
    if backward:
        section_order = section_order[::-1]
    columns = lax.all_to_all(source.T, "tok", split_axis=0, concat_axis=1, tiled=True)
    feat_rows, all_tokens = columns.shape
    field_now = columns.reshape(feat_rows, all_tokens // block_rows, block_rows)
    for section_id in section_order:
        field_now = local_section(
            field_now, mix_weights[section_id], section_bits[section_id], backward, 1
        )
    back_rows = lax.all_to_all(
        field_now.reshape(feat_rows, all_tokens), "tok", split_axis=1, concat_axis=0, tiled=True
    )
    return back_rows.T


def general_shards(tokens, mix_weights, proj_weight, pool_map, out_cot):
    tok_rows = tokens.shape[0]
    block_rows = mix_weights.shape[-1]
    section_count = mix_weights.shape[0]
    local_blocks = tok_rows // block_rows
    local_bits = local_blocks.bit_length() - 1
    tok_devices = lax.axis_size("tok")
    all_bits = local_bits + tok_devices.bit_length() - 1
    section_bits = [section_id % all_bits for section_id in range(section_count)]
    mixed = mix_tokens(tokens, mix_weights, section_bits, False)
    pool_rows = out_cot.shape[0]
    local_map = pool_map - lax.axis_index("tok") * pool_rows
    membership = (local_map[None, :] == jnp.arange(pool_rows, dtype=jnp.int32)[:, None]).astype(
        jnp.bfloat16
    )
    counts = jnp.sum(membership.astype(jnp.float32), axis=1)
    group_sums = jnp.dot(membership, mixed, preferred_element_type=jnp.float32)
    pooled = (group_sums / counts[:, None]).astype(jnp.bfloat16)
    proj_share = lax.psum_scatter(
        lax.dot_general(
            proj_weight, pooled, (((0,), (1,)), ((), ())), preferred_element_type=jnp.float32
        ).astype(jnp.bfloat16),
        "tp",
        scatter_dimension=0,
        tiled=True,
    ).astype(jnp.float32)
    projected = proj_share.T.astype(jnp.bfloat16)
    cot_full = lax.all_gather(out_cot, "tp", axis=1, tiled=True)
    d_pooled = lax.dot_general(
        cot_full, proj_weight, (((1,), (1,)), ((), ())), preferred_element_type=jnp.float32
    )
    back_rows = jnp.take(d_pooled / counts[:, None], local_map, axis=0).astype(jnp.bfloat16)
    token_grad = mix_tokens(back_rows, mix_weights, section_bits, True)
    grad_share = lax.psum_scatter(
        lax.dot_general(
            cot_full, pooled, (((0,), (0,)), ((), ())), preferred_element_type=jnp.float32
        ),
        "tok",
        scatter_dimension=0,
        tiled=True,
    )
    grad_scale = 1.0 / math.sqrt(pool_rows * tok_devices)
    proj_grad = grad_share * grad_scale
    return (projected, token_grad, proj_grad)


def one_hot(map_row, pool_rows):
    ids = lax.broadcasted_iota(jnp.int32, (pool_rows, map_row.shape[-1]), 0)
    return (map_row == ids).astype(BF16)


def run_sections(field, other, mix_ref, section_bits, backward):
    blocks, feats, rows = field.shape
    order = list(enumerate(section_bits))
    for section_id, bit in order[::-1] if backward else order:
        m = [[mix_ref[section_id, a, b] for b in range(2)] for a in range(2)]
        full = jnp.concatenate(
            [jnp.concatenate(m[0], axis=1), jnp.concatenate(m[1], axis=1)], axis=0
        )
        lows = [b for b in range(blocks) if not (b >> bit) & 1]
        step = max(1, 512 // feats)
        for at in range(0, len(lows), step):
            part = lows[at : at + step]
            low = jnp.concatenate([field[b] for b in part], axis=0)
            high = jnp.concatenate([field[b + (1 << bit)] for b in part], axis=0)
            pair = jnp.concatenate([low, high], axis=1)
            out = lax.dot_general(
                pair, full, NN if backward else NT, preferred_element_type=F32
            ).astype(BF16)
            for n, b in enumerate(part):
                other[b] = out[n * feats : (n + 1) * feats, :rows]
                other[b + (1 << bit)] = out[n * feats : (n + 1) * feats, rows:]
        field, other = other, field
    return field


def pack_kernel(pool_rows, tokens_ref, map_ref, out_ref):
    owners = out_ref.shape[0]
    blocks, rows = map_ref.shape
    feats = tokens_ref.shape[1] // owners
    maps = lax.rem(map_ref[...], jnp.int32(pool_rows)).astype(F32).astype(BF16)
    tail = jnp.concatenate([maps, jnp.zeros((TAIL - blocks, rows), BF16)], axis=0)
    for n in range(blocks):
        turned = tokens_ref[n * rows : (n + 1) * rows, :].T
        for g in range(owners):
            out_ref[g, n * feats : (n + 1) * feats, :] = turned[g * feats : (g + 1) * feats]
    for g in range(owners):
        out_ref[g, blocks * feats :, :] = tail


def hot_of(packed_ref, g, blocks, pool_rows):
    maps = packed_ref[g, packed_ref.shape[1] - TAIL :, :].astype(F32).astype(jnp.int32)
    return jnp.concatenate([one_hot(maps[n : n + 1], pool_rows) for n in range(blocks)], axis=1)


def forward_kernel(section_bits, blocks, mix_ref, packed_ref, out_ref, a_ref, b_ref):
    owners, both, pool_rows = out_ref.shape
    feats, rows = both // 2, a_ref.shape[2]
    for g in range(owners):
        for n in range(blocks):
            a_ref[g * blocks + n] = packed_ref[g, n * feats : (n + 1) * feats, :]
    done = run_sections(a_ref, b_ref, mix_ref, section_bits, False)
    ones = jnp.ones((16, blocks * rows), BF16)
    for g in range(owners):
        mine = jnp.concatenate([done[g * blocks + n] for n in range(blocks)], axis=1)
        sums = lax.dot_general(
            jnp.concatenate([mine, ones], axis=0),
            hot_of(packed_ref, g, blocks, pool_rows),
            NT,
            preferred_element_type=F32,
        )
        pooled = (sums[:feats] / sums[feats : feats + 1]).astype(BF16)
        out_ref[g, :feats, :] = pooled
        out_ref[g ^ 1, feats:, :] = pooled


def backward_kernel(section_bits, blocks, mix_ref, d_ref, packed_ref, out_ref, a_ref, b_ref):
    owners, feats, _ = out_ref.shape
    pool_rows, rows = d_ref.shape[2], a_ref.shape[2]
    for g in range(owners):
        spread = lax.dot_general(
            d_ref[g, :feats], hot_of(packed_ref, g, blocks, pool_rows), NN, preferred_element_type=F32
        ).astype(BF16)
        for n in range(blocks):
            a_ref[g * blocks + n] = spread[:, n * rows : (n + 1) * rows]
    done = run_sections(a_ref, b_ref, mix_ref, section_bits, True)
    for g in range(owners):
        for n in range(blocks):
            out_ref[g, :, n * rows : (n + 1) * rows] = done[g * blocks + n]


def unpack_kernel(grad_ref, out_ref):
    owners, _, toks = grad_ref.shape
    for at in range(0, toks, 128):
        turned = jnp.concatenate([grad_ref[g, :, at : at + 128] for g in range(owners)], axis=0)
        out_ref[at : at + 128, :] = turned.T


def early_kernel(order, w_ref, *refs):
    *cots, out_ref = refs
    outs_tp = cots[0].shape[1]
    place = lax.axis_index("tp")
    total = None
    for o, cot in zip(order, cots):
        at = pl.multiple_of((place ^ o) * outs_tp, outs_tp)
        part = lax.dot_general(
            cot[...], w_ref[:, pl.ds(at, outs_tp)], NT, preferred_element_type=F32
        )
        total = part if total is None else total + part
    out_ref[...] = total


def cotangent_kernel(groups, late, w_ref, map_ref, pooled_ref, early_ref, *refs):
    cots, out_ref, send_ref = refs[:groups], refs[groups], refs[groups + 1]
    owners, both, pool_rows = pooled_ref.shape
    feats = both // 2
    outs_tp = cots[0].shape[1]
    outs = send_ref.shape[1] // groups
    place = lax.axis_index("tp")
    other = pl.multiple_of((1 - lax.axis_index("tok") % 2) * outs, outs)
    total = early_ref[...]
    for o in late:
        at = pl.multiple_of((place ^ o) * outs_tp, outs_tp)
        total = total + lax.dot_general(
            cots[o][...], w_ref[:, pl.ds(at, outs_tp)], NT, preferred_element_type=F32
        )
    counts = jnp.zeros((pool_rows, 1), F32)
    maps = lax.rem(map_ref[...], jnp.int32(pool_rows))
    for n in range(maps.shape[0]):
        ids = lax.broadcasted_iota(jnp.int32, (pool_rows, maps.shape[1]), 0)
        hits = (maps[n : n + 1] == ids).astype(F32)
        counts = counts + jnp.sum(hits, axis=1, keepdims=True)
    turned = (total / counts).T.astype(BF16)
    for g in range(owners):
        out_ref[g, :feats, :] = turned[g * feats : (g + 1) * feats]
        out_ref[g, feats:, :] = pooled_ref[g]
    for o in range(groups):
        send_ref[:, o * outs : (o + 1) * outs] = cots[o][:, pl.ds(other, outs)]


def project_kernel(got_ref, w_ref, came_ref, *refs):
    cots, (kept_ref, sent_ref, held_ref, gone_ref) = refs[:4], refs[4:8]
    share_ref, part_ref, sems = refs[8:]
    owners, feats = got_ref.shape[0], got_ref.shape[1] // 3
    outs_tp = cots[0].shape[1]
    outs = came_ref.shape[1] // 4
    place, me = lax.axis_index("tp"), lax.axis_index("tok")
    copies = []

    def send(source, target):
        copies.append(pltpu.make_async_copy(source, target, sems.at[len(copies)]))
        copies[-1].start()

    mine = pl.multiple_of((me % 2) * outs, outs)
    turned = jnp.concatenate([got_ref[g, feats : 2 * feats, :] for g in range(owners)], axis=0)
    others = jnp.concatenate([got_ref[g, 2 * feats :, :] for g in range(owners)], axis=0)
    pooled = turned.T
    turned = jnp.concatenate([turned, others], axis=1)
    for o in (1, 3, 0, 2):
        at = pl.multiple_of((place ^ o) * outs_tp, outs_tp)
        share_ref[o] = lax.dot_general(
            pooled, w_ref[:, pl.ds(at, outs_tp)], NN, preferred_element_type=F32
        ).astype(BF16)
        send(share_ref.at[o], (sent_ref if o % 2 else kept_ref).at[o // 2])
    for o in range(4):
        cot = jnp.concatenate(
            [cots[o][:, pl.ds(mine, outs)], came_ref[:, o * outs : (o + 1) * outs]], axis=0
        )
        part_ref[place ^ o] = lax.dot_general(
            turned, cot, NN, preferred_element_type=F32
        ).astype(BF16)
    for o in (1, 3, 0, 2):
        send(part_ref.at[(me // 2) ^ o], (gone_ref if o % 2 else held_ref).at[o // 2])
    for copy in copies:
        copy.wait()


def fold_kernel(kept_ref, got_ref, held_ref, came_ref, share_ref, part_ref):
    share_ref[...] = (kept_ref[1].astype(F32) + got_ref[1].astype(F32)).astype(BF16)
    part_ref[...] = (held_ref[1].astype(F32) + came_ref[1].astype(F32)).astype(BF16)


def sum_kernel(scale, kept_ref, got_ref, share_ref, held_ref, came_ref, part_ref, projected_ref, grad_ref):
    total = kept_ref[0].astype(F32) + got_ref[0].astype(F32) + share_ref[...].astype(F32)
    projected_ref[...] = total.astype(BF16)
    total = held_ref[0].astype(F32) + came_ref[0].astype(F32) + part_ref[...].astype(F32)
    grad_ref[...] = total.T * scale


def call(kernel, operands, out_shape, scratch, name, cost=0, out_space=pltpu.VMEM):
    several = isinstance(out_shape, (list, tuple))
    vmem = pl.BlockSpec(memory_space=pltpu.VMEM)
    out = pl.BlockSpec(memory_space=out_space)
    return pl.pallas_call(
        kernel,
        out_shape=out_shape,
        in_specs=[vmem] * len(operands),
        out_specs=[out] * len(out_shape) if several else out,
        scratch_shapes=scratch,
        compiler_params=pltpu.CompilerParams(vmem_limit_bytes=VMEM_LIMIT),
        cost_estimate=pl.CostEstimate(flops=cost, bytes_accessed=0, transcendentals=0),
        name=name,
    )(*operands)


def struct(*shape, dtype=BF16):
    return jax.ShapeDtypeStruct(shape, dtype)


def in_hbm(*shape, dtype=BF16):
    return pltpu.HBM(shape, dtype)


def swap(piece, axis, offset):
    size = lax.axis_size(axis)
    return lax.ppermute(piece, axis, [(i, i ^ offset) for i in range(size)])


def swap_all(pieces, axis):
    return [pieces[0]] + [swap(piece, axis, o) for o, piece in enumerate(pieces) if o]


def exchange(pieces, axis):
    return lax.all_to_all(pieces, axis, split_axis=0, concat_axis=0, tiled=True)


def shards(tokens, mix_weights, proj_weight, pool_map, out_cot):
    toks, feats_tp = tokens.shape
    section_count, rows = mix_weights.shape[0], mix_weights.shape[-1]
    owners, groups = lax.axis_size("tok"), lax.axis_size("tp")
    pool_rows, outs_tp = out_cot.shape
    outs = outs_tp * groups // owners
    feats = feats_tp // owners
    blocks = toks // rows
    if feats % 16 or outs % 128 or owners != 8 or groups != 4 or pool_rows > 256 or blocks > TAIL:
        return general_shards(tokens, mix_weights, proj_weight, pool_map, out_cot)
    all_bits = (owners * blocks).bit_length() - 1
    section_bits = [section_id % all_bits for section_id in range(section_count)]
    fields = [pltpu.VMEM((owners * blocks, feats, rows), BF16)] * 2

    cots = [out_cot] + [swap(out_cot, "tp", o) for o in range(1, groups)]
    maps = pool_map.reshape(blocks, rows)
    packed = call(
        functools.partial(pack_kernel, pool_rows),
        (tokens, maps),
        struct(owners, blocks * feats + TAIL, rows),
        [],
        "pack",
    )
    packed = exchange(packed, "tok")
    order = [0] + list(range(2, groups))
    early = call(
        functools.partial(early_kernel, order),
        (proj_weight, *[cots[o] for o in order]),
        struct(pool_rows, feats_tp, dtype=F32),
        [],
        "early_cotangent",
        LONG,
    )
    packed, early = lax.optimization_barrier((packed, early))
    pooled = call(
        functools.partial(forward_kernel, section_bits, blocks),
        (mix_weights, packed),
        struct(owners, 2 * feats, pool_rows),
        fields,
        "forward_mix",
    )
    both, half = call(
        functools.partial(cotangent_kernel, groups, [1]),
        (proj_weight, maps, pooled, early, *cots),
        [struct(owners, 3 * feats, pool_rows), struct(pool_rows, groups * outs)],
        [],
        "cotangent",
    )
    half = swap(half, "tok", 1)
    both = exchange(both, "tok")

    kept, sent, held, gone = call(
        project_kernel,
        (both, proj_weight, half, *cots),
        [in_hbm(2, pool_rows, outs_tp)] * 2 + [in_hbm(2, feats_tp, outs)] * 2,
        [
            pltpu.VMEM((4, pool_rows, outs_tp), BF16),
            pltpu.VMEM((4, feats_tp, outs), BF16),
            pltpu.SemaphoreType.DMA((8,)),
        ],
        "project",
        out_space=pltpu.HBM,
    )
    sent, gone = swap(sent, "tp", 1), swap(gone, "tok", 2)
    share, part = call(
        fold_kernel,
        (kept, sent, held, gone),
        [struct(pool_rows, outs_tp), struct(feats_tp, outs)],
        [],
        "fold",
        LONG,
    )
    share, part = swap(share, "tp", 2), swap(part, "tok", 4)
    projected, proj_grad = call(
        functools.partial(sum_kernel, 1.0 / math.sqrt(pool_rows * owners)),
        (kept, sent, share, held, gone, part),
        [struct(pool_rows, outs_tp), struct(outs, feats_tp, dtype=F32)],
        [],
        "sums",
    )

    grad = call(
        functools.partial(backward_kernel, section_bits, blocks),
        (mix_weights, both, packed),
        struct(owners, feats, toks),
        fields,
        "backward_mix",
    )
    grad = exchange(grad, "tok")
    token_grad = call(unpack_kernel, (grad,), struct(toks, feats_tp), [], "unpack")
    return (projected, token_grad, proj_grad)


def solution(mesh):
    in_specs = (P("tok", "tp"), P(), P("tp", None), P("tok"), P("tok", "tp"))
    out_specs = (P("tok", "tp"), P("tok", "tp"), P("tok", "tp"))
    return jax.shard_map(shards, mesh=mesh, in_specs=in_specs, out_specs=out_specs, check_vma=False)
```

```python
import functools
import math

import jax
import jax.numpy as jnp
from jax import lax
from jax.experimental import pallas as pl
from jax.experimental.pallas import tpu as pltpu
from jax.sharding import PartitionSpec as P

F32 = jnp.float32
BF16 = jnp.bfloat16
VMEM_LIMIT = 40 * 1024 * 1024
NT = (((1,), (1,)), ((), ()))
NN = (((1,), (0,)), ((), ()))
TAIL = 16
LONG = 30_000_000_000
RELAY = 5_000_000_000
SUMS = 1_500_000_000


def contract(matrix, operand, backward):
    pattern = "ji,...j->...i" if backward else "ij,...j->...i"
    return jnp.einsum(pattern, matrix, operand, preferred_element_type=jnp.float32)


def local_section(field_now, section_mats, bit_index, backward, block_axis):
    full_shape = field_now.shape
    nblocks = full_shape[block_axis]
    split_shape = (
        full_shape[:block_axis]
        + (nblocks >> bit_index + 1, 2, 1 << bit_index)
        + full_shape[block_axis + 1 :]
    )
    paired = field_now.reshape(split_shape)
    lower_half = lax.index_in_dim(paired, 0, block_axis + 1, keepdims=False)
    upper_half = lax.index_in_dim(paired, 1, block_axis + 1, keepdims=False)
    if backward:
        new_lower = contract(section_mats[0, 0], lower_half, True) + contract(
            section_mats[1, 0], upper_half, True
        )
        new_upper = contract(section_mats[0, 1], lower_half, True) + contract(
            section_mats[1, 1], upper_half, True
        )
    else:
        new_lower = contract(section_mats[0, 0], lower_half, False) + contract(
            section_mats[0, 1], upper_half, False
        )
        new_upper = contract(section_mats[1, 0], lower_half, False) + contract(
            section_mats[1, 1], upper_half, False
        )
    joined = jnp.stack(
        [new_lower.astype(jnp.bfloat16), new_upper.astype(jnp.bfloat16)], axis=block_axis + 1
    )
    return joined.reshape(full_shape)


def mix_tokens(source, mix_weights, section_bits, backward):
    block_rows = mix_weights.shape[-1]
    section_order = list(range(len(section_bits)))
    if backward:
        section_order = section_order[::-1]
    columns = lax.all_to_all(source.T, "tok", split_axis=0, concat_axis=1, tiled=True)
    feat_rows, all_tokens = columns.shape
    field_now = columns.reshape(feat_rows, all_tokens // block_rows, block_rows)
    for section_id in section_order:
        field_now = local_section(
            field_now, mix_weights[section_id], section_bits[section_id], backward, 1
        )
    back_rows = lax.all_to_all(
        field_now.reshape(feat_rows, all_tokens), "tok", split_axis=1, concat_axis=0, tiled=True
    )
    return back_rows.T


def general_shards(tokens, mix_weights, proj_weight, pool_map, out_cot):
    tok_rows = tokens.shape[0]
    block_rows = mix_weights.shape[-1]
    section_count = mix_weights.shape[0]
    local_blocks = tok_rows // block_rows
    local_bits = local_blocks.bit_length() - 1
    tok_devices = lax.axis_size("tok")
    all_bits = local_bits + tok_devices.bit_length() - 1
    section_bits = [section_id % all_bits for section_id in range(section_count)]
    mixed = mix_tokens(tokens, mix_weights, section_bits, False)
    pool_rows = out_cot.shape[0]
    local_map = pool_map - lax.axis_index("tok") * pool_rows
    membership = (local_map[None, :] == jnp.arange(pool_rows, dtype=jnp.int32)[:, None]).astype(
        jnp.bfloat16
    )
    counts = jnp.sum(membership.astype(jnp.float32), axis=1)
    group_sums = jnp.dot(membership, mixed, preferred_element_type=jnp.float32)
    pooled = (group_sums / counts[:, None]).astype(jnp.bfloat16)
    proj_share = lax.psum_scatter(
        lax.dot_general(
            proj_weight, pooled, (((0,), (1,)), ((), ())), preferred_element_type=jnp.float32
        ).astype(jnp.bfloat16),
        "tp",
        scatter_dimension=0,
        tiled=True,
    ).astype(jnp.float32)
    projected = proj_share.T.astype(jnp.bfloat16)
    cot_full = lax.all_gather(out_cot, "tp", axis=1, tiled=True)
    d_pooled = lax.dot_general(
        cot_full, proj_weight, (((1,), (1,)), ((), ())), preferred_element_type=jnp.float32
    )
    back_rows = jnp.take(d_pooled / counts[:, None], local_map, axis=0).astype(jnp.bfloat16)
    token_grad = mix_tokens(back_rows, mix_weights, section_bits, True)
    grad_share = lax.psum_scatter(
        lax.dot_general(
            cot_full, pooled, (((0,), (0,)), ((), ())), preferred_element_type=jnp.float32
        ),
        "tok",
        scatter_dimension=0,
        tiled=True,
    )
    grad_scale = 1.0 / math.sqrt(pool_rows * tok_devices)
    proj_grad = grad_share * grad_scale
    return (projected, token_grad, proj_grad)


def one_hot(map_row, pool_rows):
    ids = lax.broadcasted_iota(jnp.int32, (pool_rows, map_row.shape[-1]), 0)
    return (map_row == ids).astype(BF16)


def run_sections(field, other, mix_ref, section_bits, backward):
    blocks, feats, rows = field.shape
    order = list(enumerate(section_bits))
    for section_id, bit in order[::-1] if backward else order:
        m = [[mix_ref[section_id, a, b] for b in range(2)] for a in range(2)]
        full = jnp.concatenate(
            [jnp.concatenate(m[0], axis=1), jnp.concatenate(m[1], axis=1)], axis=0
        )
        lows = [b for b in range(blocks) if not (b >> bit) & 1]
        step = max(1, 512 // feats)
        for at in range(0, len(lows), step):
            part = lows[at : at + step]
            low = jnp.concatenate([field[b] for b in part], axis=0)
            high = jnp.concatenate([field[b + (1 << bit)] for b in part], axis=0)
            pair = jnp.concatenate([low, high], axis=1)
            out = lax.dot_general(
                pair, full, NN if backward else NT, preferred_element_type=F32
            ).astype(BF16)
            for n, b in enumerate(part):
                other[b] = out[n * feats : (n + 1) * feats, :rows]
                other[b + (1 << bit)] = out[n * feats : (n + 1) * feats, rows:]
        field, other = other, field
    return field


def pack_kernel(pool_rows, tokens_ref, map_ref, *refs):
    outs, (held_ref, maps_ref, packed_ref, sems) = refs[:4], refs[4:]
    blocks, rows = map_ref.shape
    owners = packed_ref.shape[0]
    feats = tokens_ref.shape[2] // owners
    loads = [
        pltpu.make_async_copy(tokens_ref.at[n], held_ref.at[n], sems.at[n]) for n in range(blocks)
    ]
    loads.append(pltpu.make_async_copy(map_ref, maps_ref, sems.at[blocks]))
    for load in loads:
        load.start()
    loads[blocks].wait()
    maps = lax.rem(maps_ref[...], jnp.int32(pool_rows)).astype(F32).astype(BF16)
    tail = jnp.concatenate([maps, jnp.zeros((TAIL - blocks, rows), BF16)], axis=0)
    for g in range(owners):
        packed_ref[g, blocks * feats :, :] = tail
    for n in range(blocks):
        loads[n].wait()
        turned = held_ref[n].T
        for g in range(owners):
            packed_ref[g, n * feats : (n + 1) * feats, :] = turned[g * feats : (g + 1) * feats]
    chip = lax.axis_index("tok") // 2
    for o in range(4):
        outs[o][...] = packed_ref[pl.ds((chip ^ o) * 2, 2)]


def hot_of(maps, pool_rows):
    maps = maps.astype(F32).astype(jnp.int32)
    return jnp.concatenate(
        [one_hot(maps[n : n + 1], pool_rows) for n in range(maps.shape[0])], axis=1
    )


def sources(pieces):
    me = lax.axis_index("tok")
    for k, piece in enumerate(pieces):
        yield me ^ (2 * (k % 4) + k // 4), piece


def forward_kernel(section_bits, blocks, mix_ref, *refs):
    pieces, (out_ref, map_ref, a_ref, b_ref) = refs[:8], refs[8:]
    owners, feats, pool_rows = out_ref.shape
    rows = a_ref.shape[2]
    core = lax.axis_index("tok") % 2
    for g, piece in sources(pieces):
        map_ref[g] = piece[core, blocks * feats :, :]
        for n in range(blocks):
            a_ref[g * blocks + n] = piece[core, n * feats : (n + 1) * feats, :]
    done = run_sections(a_ref, b_ref, mix_ref, section_bits, False)
    ones = jnp.ones((16, blocks * rows), BF16)
    for g in range(owners):
        mine = jnp.concatenate([done[g * blocks + n] for n in range(blocks)], axis=1)
        sums = lax.dot_general(
            jnp.concatenate([mine, ones], axis=0),
            hot_of(map_ref[g][:blocks], pool_rows),
            NT,
            preferred_element_type=F32,
        )
        out_ref[g] = (sums[:feats] / sums[feats : feats + 1]).astype(BF16)


def backward_kernel(section_bits, blocks, mix_ref, map_ref, *refs):
    pieces, outs, (a_ref, b_ref, d_ref) = refs[:8], refs[8:12], refs[12:]
    owners, feats, pool_rows = d_ref.shape
    rows = a_ref.shape[2]
    me = lax.axis_index("tok")
    for g, piece in sources(pieces):
        d_ref[g] = piece[me % 2, :feats]
    for g in range(owners):
        spread = lax.dot_general(
            d_ref[g], hot_of(map_ref[g][:blocks], pool_rows), NN, preferred_element_type=F32
        ).astype(BF16)
        for n in range(blocks):
            a_ref[g * blocks + n] = spread[:, n * rows : (n + 1) * rows]
    done = run_sections(a_ref, b_ref, mix_ref, section_bits, True)
    for o in range(4):
        outs[o][...] = done[pl.ds((me // 2 ^ o) * 2 * blocks, 2 * blocks)]


def unpack_kernel(*refs):
    pieces, out_ref, all_ref = refs[:8], refs[8], refs[9]
    blocks, feats, rows = pieces[0].shape[0] // 2, *pieces[0].shape[1:]
    core = lax.axis_index("tok") % 2
    for g, piece in sources(pieces):
        at = pl.ds(pl.multiple_of(g * feats, feats), feats)
        all_ref[:, at, :] = piece[pl.ds(core * blocks, blocks)]
    for n in range(blocks):
        out_ref[n * rows : (n + 1) * rows, :] = all_ref[n].T


def relay_kernel(came_ref, *refs):
    refs[-1][...] = came_ref[...]


def early_kernel(w_ref, own_ref, came_ref, out_ref):
    outs_tp = own_ref.shape[1]
    place = lax.axis_index("tp")
    total = None
    for o, cot in ((0, own_ref), (2, came_ref)):
        at = pl.multiple_of((place ^ o) * outs_tp, outs_tp)
        part = lax.dot_general(
            cot[...], w_ref[:, pl.ds(at, outs_tp)], NT, preferred_element_type=F32
        )
        total = part if total is None else total + part
    out_ref[...] = total


def cotangent_kernel(w_ref, map_ref, pooled_ref, early_ref, *refs):
    cots, outs_ref, (send_ref, turned_ref) = refs[:4], refs[4:8], refs[8:]
    owners, feats, pool_rows = pooled_ref.shape
    outs_tp = cots[0].shape[1]
    outs = send_ref.shape[1] // 4
    place, me = lax.axis_index("tp"), lax.axis_index("tok")
    other = pl.multiple_of((1 - me % 2) * outs, outs)
    total = early_ref[...]
    for o in (1, 3):
        at = pl.multiple_of((place ^ o) * outs_tp, outs_tp)
        total = total + lax.dot_general(
            cots[o][...], w_ref[:, pl.ds(at, outs_tp)], NT, preferred_element_type=F32
        )
    counts = jnp.zeros((pool_rows, 1), F32)
    maps = lax.rem(map_ref[...], jnp.int32(pool_rows))
    for n in range(maps.shape[0]):
        ids = lax.broadcasted_iota(jnp.int32, (pool_rows, maps.shape[1]), 0)
        hits = (maps[n : n + 1] == ids).astype(F32)
        counts = counts + jnp.sum(hits, axis=1, keepdims=True)
    turned = (total / counts).T.astype(BF16)
    for g in range(owners):
        turned_ref[g] = turned[g * feats : (g + 1) * feats]
    for o in range(4):
        for core in range(2):
            g = (me // 2 ^ o) * 2 + core
            outs_ref[o][core, :feats, :] = turned_ref[g]
            outs_ref[o][core, feats:, :] = pooled_ref[g]
    for o in range(4):
        send_ref[:, o * outs : (o + 1) * outs] = cots[o][:, pl.ds(other, outs)]


def project_kernel(w_ref, came_ref, *refs):
    cots, pieces, shares, (held_ref, gone_ref) = refs[:4], refs[4:12], refs[12:16], refs[16:18]
    share_ref, part_ref, pool_ref, sems = refs[18:]
    feats, pool_rows = pieces[0].shape[1] // 2, pieces[0].shape[2]
    outs_tp = cots[0].shape[1]
    outs = came_ref.shape[1] // 4
    place, me = lax.axis_index("tp"), lax.axis_index("tok")
    copies = []

    def send(source, target):
        copies.append(pltpu.make_async_copy(source, target, sems.at[len(copies)]))
        copies[-1].start()

    mine = pl.multiple_of((me % 2) * outs, outs)
    for g, piece in sources(pieces):
        pool_ref[g, :, :pool_rows] = piece[me % 2, feats:, :]
        pool_ref[g, :, pool_rows:] = piece[1 - me % 2, feats:, :]
    turned = jnp.concatenate([pool_ref[g] for g in range(len(pieces))], axis=0)
    pooled = turned[:, :pool_rows].T
    for o in (3, 1, 2, 0):
        at = pl.multiple_of((place ^ o) * outs_tp, outs_tp)
        share_ref[o] = lax.dot_general(
            pooled, w_ref[:, pl.ds(at, outs_tp)], NN, preferred_element_type=F32
        ).astype(BF16)
        send(share_ref.at[o], shares[o])
    for o in range(4):
        own = cots[o][:, pl.ds(mine, outs)]
        cot = jnp.concatenate(
            [own, came_ref[:, o * outs : (o + 1) * outs]], axis=0
        )
        part_ref[place ^ o] = lax.dot_general(
            turned, cot, NN, preferred_element_type=F32
        ).astype(BF16)
    for o in (1, 3, 0, 2):
        send(part_ref.at[(me // 2) ^ o], (gone_ref if o % 2 else held_ref).at[o // 2])
    for copy in copies:
        copy.wait()


def fold_kernel(kept_ref, got_ref, held_ref, came_ref, share_ref, part_ref):
    share_ref[...] = (kept_ref[...].astype(F32) + got_ref[...].astype(F32)).astype(BF16)
    part_ref[...] = (held_ref[1].astype(F32) + came_ref[1].astype(F32)).astype(BF16)


def sum_kernel(scale, kept_ref, got_ref, share_ref, held_ref, came_ref, part_ref, projected_ref, grad_ref):
    total = kept_ref[...].astype(F32) + got_ref[...].astype(F32) + share_ref[...].astype(F32)
    projected_ref[...] = total.astype(BF16)
    total = held_ref[0].astype(F32) + came_ref[0].astype(F32) + part_ref[...].astype(F32)
    grad_ref[...] = total.T * scale


def call(kernel, operands, out_shape, scratch, name, cost=0, out_space=pltpu.VMEM, in_space=pltpu.VMEM):
    several = isinstance(out_shape, (list, tuple))
    into = pl.BlockSpec(memory_space=in_space)
    if in_space == pltpu.HBM:
        operands = [pltpu.with_memory_space_constraint(a, pltpu.HBM) for a in operands]
    spaces = out_space if isinstance(out_space, tuple) else (out_space,) * (len(out_shape) if several else 1)
    out = [pl.BlockSpec(memory_space=space) for space in spaces]
    return pl.pallas_call(
        kernel,
        out_shape=out_shape,
        in_specs=[into] * len(operands),
        out_specs=out if several else out[0],
        scratch_shapes=scratch,
        compiler_params=pltpu.CompilerParams(vmem_limit_bytes=VMEM_LIMIT),
        cost_estimate=pl.CostEstimate(flops=cost, bytes_accessed=0, transcendentals=0),
        name=name,
    )(*operands)


def struct(*shape, dtype=BF16):
    return jax.ShapeDtypeStruct(shape, dtype)


def in_hbm(*shape, dtype=BF16):
    return pltpu.HBM(shape, dtype)


def swap(piece, axis, offset):
    size = lax.axis_size(axis)
    return lax.ppermute(piece, axis, [(i, i ^ offset) for i in range(size)])


def swap_all(pieces, axis):
    return [pieces[0]] + [swap(piece, axis, o) for o, piece in enumerate(pieces) if o]


def exchange(pieces):
    came = [pieces[0]] + [swap(pieces[o], "tok", 2 * o) for o in (1, 2, 3)]
    return came + [swap(piece, "tok", 1) for piece in came]


def shards(tokens, mix_weights, proj_weight, pool_map, out_cot):
    toks, feats_tp = tokens.shape
    section_count, rows = mix_weights.shape[0], mix_weights.shape[-1]
    owners, groups = lax.axis_size("tok"), lax.axis_size("tp")
    pool_rows, outs_tp = out_cot.shape
    outs = outs_tp * groups // owners
    feats = feats_tp // owners
    blocks = toks // rows
    if feats % 16 or outs % 128 or owners != 8 or groups != 4 or pool_rows > 256 or blocks > TAIL:
        return general_shards(tokens, mix_weights, proj_weight, pool_map, out_cot)
    all_bits = (owners * blocks).bit_length() - 1
    section_bits = [section_id % all_bits for section_id in range(section_count)]
    fields = [pltpu.VMEM((owners * blocks, feats, rows), BF16)] * 2

    across = swap(out_cot, "tp", 2)
    beside = swap(out_cot, "tp", 1)
    onward = call(relay_kernel, (across, beside), struct(pool_rows, outs_tp), [], "relay", RELAY)
    cots = [out_cot, beside, across, swap(onward, "tp", 1)]
    maps = pool_map.reshape(blocks, rows)
    height = blocks * feats + TAIL
    packed = call(
        functools.partial(pack_kernel, pool_rows),
        (tokens.reshape(blocks, rows, feats_tp), maps),
        [struct(2, height, rows)] * 4,
        [
            pltpu.VMEM((blocks, rows, feats_tp), BF16),
            pltpu.VMEM((blocks, rows), jnp.int32),
            pltpu.VMEM((owners, height, rows), BF16),
            pltpu.SemaphoreType.DMA((blocks + 1,)),
        ],
        "pack",
        in_space=pltpu.HBM,
    )
    packed = exchange(packed)
    early = call(
        early_kernel,
        (proj_weight, out_cot, across),
        struct(pool_rows, feats_tp, dtype=F32),
        [],
        "early_cotangent",
    )
    pooled, map_rows = call(
        functools.partial(forward_kernel, section_bits, blocks),
        (mix_weights, *packed),
        [struct(owners, feats, pool_rows), struct(owners, TAIL, rows)],
        fields,
        "forward_mix",
    )
    *both, half = call(
        cotangent_kernel,
        (proj_weight, maps, pooled, early, *cots),
        [struct(2, 2 * feats, pool_rows)] * 4 + [struct(pool_rows, groups * outs)],
        [pltpu.VMEM((owners, feats, pool_rows), BF16)],
        "cotangent",
    )
    half = swap(half, "tok", 1)
    both = exchange(both)

    *shares, held, gone = call(
        project_kernel,
        (proj_weight, half, *cots, *both),
        [in_hbm(pool_rows, outs_tp)] * 4 + [in_hbm(2, feats_tp, outs)] * 2,
        [
            pltpu.VMEM((4, pool_rows, outs_tp), BF16),
            pltpu.VMEM((4, feats_tp, outs), BF16),
            pltpu.VMEM((owners, feats, 2 * pool_rows), BF16),
            pltpu.SemaphoreType.DMA((8,)),
        ],
        "project",
        out_space=pltpu.HBM,
    )
    gone = swap(gone, "tok", 2)
    share, part = call(
        fold_kernel,
        (shares[2], swap(shares[3], "tp", 1), held, gone),
        [struct(pool_rows, outs_tp), struct(feats_tp, outs)],
        [],
        "fold",
        LONG,
    )
    kept, sent, share = shares[0], swap(shares[1], "tp", 1), swap(share, "tp", 2)
    part = swap(part, "tok", 4)
    projected, proj_grad = call(
        functools.partial(sum_kernel, 1.0 / math.sqrt(pool_rows * owners)),
        (kept, sent, share, held, gone, part),
        [struct(pool_rows, outs_tp), struct(outs, feats_tp, dtype=F32)],
        [],
        "sums",
        SUMS,
    )

    grad = call(
        functools.partial(backward_kernel, section_bits, blocks),
        (mix_weights, map_rows, *both),
        [struct(2 * blocks, feats, rows)] * 4,
        fields + [pltpu.VMEM((owners, feats, pool_rows), BF16)],
        "backward_mix",
    )
    grad, projected = lax.optimization_barrier((exchange(grad), projected))
    token_grad = call(
        unpack_kernel,
        grad,
        struct(toks, feats_tp),
        [pltpu.VMEM((blocks, feats_tp, rows), BF16)],
        "unpack",
    )
    return (projected, token_grad, proj_grad)


def solution(mesh):
    in_specs = (P("tok", "tp"), P(), P("tp", None), P("tok"), P("tok", "tp"))
    out_specs = (P("tok", "tp"), P("tok", "tp"), P("tok", "tp"))
    return jax.shard_map(shards, mesh=mesh, in_specs=in_specs, out_specs=out_specs, check_vma=False)
```

```python
import functools
import math

import jax
import jax.numpy as jnp
from jax import lax
from jax.experimental import pallas as pl
from jax.experimental.pallas import tpu as pltpu
from jax.sharding import PartitionSpec as P

F32 = jnp.float32
BF16 = jnp.bfloat16
VMEM_LIMIT = 40 * 1024 * 1024
NT = (((1,), (1,)), ((), ()))
NN = (((1,), (0,)), ((), ()))
TAIL = 16
RELAY = 5_000_000_000
SUMS = 1_500_000_000


def contract(matrix, operand, backward):
    pattern = "ji,...j->...i" if backward else "ij,...j->...i"
    return jnp.einsum(pattern, matrix, operand, preferred_element_type=jnp.float32)


def local_section(field_now, section_mats, bit_index, backward, block_axis):
    full_shape = field_now.shape
    nblocks = full_shape[block_axis]
    split_shape = (
        full_shape[:block_axis]
        + (nblocks >> bit_index + 1, 2, 1 << bit_index)
        + full_shape[block_axis + 1 :]
    )
    paired = field_now.reshape(split_shape)
    lower_half = lax.index_in_dim(paired, 0, block_axis + 1, keepdims=False)
    upper_half = lax.index_in_dim(paired, 1, block_axis + 1, keepdims=False)
    if backward:
        new_lower = contract(section_mats[0, 0], lower_half, True) + contract(
            section_mats[1, 0], upper_half, True
        )
        new_upper = contract(section_mats[0, 1], lower_half, True) + contract(
            section_mats[1, 1], upper_half, True
        )
    else:
        new_lower = contract(section_mats[0, 0], lower_half, False) + contract(
            section_mats[0, 1], upper_half, False
        )
        new_upper = contract(section_mats[1, 0], lower_half, False) + contract(
            section_mats[1, 1], upper_half, False
        )
    joined = jnp.stack(
        [new_lower.astype(jnp.bfloat16), new_upper.astype(jnp.bfloat16)], axis=block_axis + 1
    )
    return joined.reshape(full_shape)


def mix_tokens(source, mix_weights, section_bits, backward):
    block_rows = mix_weights.shape[-1]
    section_order = list(range(len(section_bits)))
    if backward:
        section_order = section_order[::-1]
    columns = lax.all_to_all(source.T, "tok", split_axis=0, concat_axis=1, tiled=True)
    feat_rows, all_tokens = columns.shape
    field_now = columns.reshape(feat_rows, all_tokens // block_rows, block_rows)
    for section_id in section_order:
        field_now = local_section(
            field_now, mix_weights[section_id], section_bits[section_id], backward, 1
        )
    back_rows = lax.all_to_all(
        field_now.reshape(feat_rows, all_tokens), "tok", split_axis=1, concat_axis=0, tiled=True
    )
    return back_rows.T


def general_shards(tokens, mix_weights, proj_weight, pool_map, out_cot):
    tok_rows = tokens.shape[0]
    block_rows = mix_weights.shape[-1]
    section_count = mix_weights.shape[0]
    local_blocks = tok_rows // block_rows
    local_bits = local_blocks.bit_length() - 1
    tok_devices = lax.axis_size("tok")
    all_bits = local_bits + tok_devices.bit_length() - 1
    section_bits = [section_id % all_bits for section_id in range(section_count)]
    mixed = mix_tokens(tokens, mix_weights, section_bits, False)
    pool_rows = out_cot.shape[0]
    local_map = pool_map - lax.axis_index("tok") * pool_rows
    membership = (local_map[None, :] == jnp.arange(pool_rows, dtype=jnp.int32)[:, None]).astype(
        jnp.bfloat16
    )
    counts = jnp.sum(membership.astype(jnp.float32), axis=1)
    group_sums = jnp.dot(membership, mixed, preferred_element_type=jnp.float32)
    pooled = (group_sums / counts[:, None]).astype(jnp.bfloat16)
    proj_share = lax.psum_scatter(
        lax.dot_general(
            proj_weight, pooled, (((0,), (1,)), ((), ())), preferred_element_type=jnp.float32
        ).astype(jnp.bfloat16),
        "tp",
        scatter_dimension=0,
        tiled=True,
    ).astype(jnp.float32)
    projected = proj_share.T.astype(jnp.bfloat16)
    cot_full = lax.all_gather(out_cot, "tp", axis=1, tiled=True)
    d_pooled = lax.dot_general(
        cot_full, proj_weight, (((1,), (1,)), ((), ())), preferred_element_type=jnp.float32
    )
    back_rows = jnp.take(d_pooled / counts[:, None], local_map, axis=0).astype(jnp.bfloat16)
    token_grad = mix_tokens(back_rows, mix_weights, section_bits, True)
    grad_share = lax.psum_scatter(
        lax.dot_general(
            cot_full, pooled, (((0,), (0,)), ((), ())), preferred_element_type=jnp.float32
        ),
        "tok",
        scatter_dimension=0,
        tiled=True,
    )
    grad_scale = 1.0 / math.sqrt(pool_rows * tok_devices)
    proj_grad = grad_share * grad_scale
    return (projected, token_grad, proj_grad)


def one_hot(map_row, pool_rows):
    ids = lax.broadcasted_iota(jnp.int32, (pool_rows, map_row.shape[-1]), 0)
    return (map_row == ids).astype(BF16)


def run_sections(field, other, mix_ref, section_bits, backward):
    blocks, feats, rows = field.shape
    order = list(enumerate(section_bits))
    for section_id, bit in order[::-1] if backward else order:
        m = [[mix_ref[section_id, a, b] for b in range(2)] for a in range(2)]
        full = jnp.concatenate(
            [jnp.concatenate(m[0], axis=1), jnp.concatenate(m[1], axis=1)], axis=0
        )
        lows = [b for b in range(blocks) if not (b >> bit) & 1]
        step = max(1, 512 // feats)
        for at in range(0, len(lows), step):
            part = lows[at : at + step]
            low = jnp.concatenate([field[b] for b in part], axis=0)
            high = jnp.concatenate([field[b + (1 << bit)] for b in part], axis=0)
            pair = jnp.concatenate([low, high], axis=1)
            out = lax.dot_general(
                pair, full, NN if backward else NT, preferred_element_type=F32
            ).astype(BF16)
            for n, b in enumerate(part):
                other[b] = out[n * feats : (n + 1) * feats, :rows]
                other[b + (1 << bit)] = out[n * feats : (n + 1) * feats, rows:]
        field, other = other, field
    return field


def pack_kernel(pool_rows, tokens_ref, map_ref, *refs):
    outs, (held_ref, maps_ref, packed_ref, sems) = refs[:4], refs[4:]
    blocks, rows = map_ref.shape
    owners = packed_ref.shape[0]
    feats = tokens_ref.shape[2] // owners
    loads = [
        pltpu.make_async_copy(tokens_ref.at[n], held_ref.at[n], sems.at[n]) for n in range(blocks)
    ]
    loads.append(pltpu.make_async_copy(map_ref, maps_ref, sems.at[blocks]))
    for load in loads:
        load.start()
    loads[blocks].wait()
    maps = lax.rem(maps_ref[...], jnp.int32(pool_rows)).astype(F32).astype(BF16)
    tail = jnp.concatenate([maps, jnp.zeros((TAIL - blocks, rows), BF16)], axis=0)
    for g in range(owners):
        packed_ref[g, blocks * feats :, :] = tail
    for n in range(blocks):
        loads[n].wait()
        turned = held_ref[n].T
        for g in range(owners):
            packed_ref[g, n * feats : (n + 1) * feats, :] = turned[g * feats : (g + 1) * feats]
    chip = lax.axis_index("tok") // 2
    for o in range(4):
        outs[o][...] = packed_ref[pl.ds((chip ^ o) * 2, 2)]


def hot_of(maps, pool_rows):
    maps = maps.astype(F32).astype(jnp.int32)
    return jnp.concatenate(
        [one_hot(maps[n : n + 1], pool_rows) for n in range(maps.shape[0])], axis=1
    )


def sources(pieces):
    me = lax.axis_index("tok")
    if len(pieces) == 8:
        for k, piece in enumerate(pieces):
            yield me ^ (2 * (k % 4) + k // 4), piece, me % 2
        return
    for k, piece in enumerate(pieces[:4]):
        yield me ^ (2 * k), piece, me % 2
    for k in range(3):
        yield me ^ (2 * k + 1), pieces[4].at[k], 0
    yield me ^ 7, pieces[5], me % 2


def gather_kernel(*refs):
    *pieces, out_ref = refs
    count = out_ref.shape[1]
    other = 1 - lax.axis_index("tok") % 2
    for k, piece in enumerate(pieces):
        out_ref[k] = piece[pl.ds(other * count, count)]


def forward_kernel(section_bits, blocks, mix_ref, *refs):
    pieces, (out_ref, map_ref, a_ref, b_ref) = refs[:6], refs[6:]
    owners, feats, pool_rows = out_ref.shape
    rows = a_ref.shape[2]
    for g, piece, at in sources(pieces):
        map_ref[g] = piece[at, blocks * feats :, :]
        for n in range(blocks):
            a_ref[g * blocks + n] = piece[at, n * feats : (n + 1) * feats, :]
    done = run_sections(a_ref, b_ref, mix_ref, section_bits, False)
    ones = jnp.ones((16, blocks * rows), BF16)
    for g in range(owners):
        mine = jnp.concatenate([done[g * blocks + n] for n in range(blocks)], axis=1)
        sums = lax.dot_general(
            jnp.concatenate([mine, ones], axis=0),
            hot_of(map_ref[g][:blocks], pool_rows),
            NT,
            preferred_element_type=F32,
        )
        out_ref[g] = (sums[:feats] / sums[feats : feats + 1]).astype(BF16)


def backward_kernel(section_bits, blocks, mix_ref, map_ref, *refs):
    pieces, outs, (a_ref, b_ref, d_ref) = refs[:8], refs[8:12], refs[12:]
    owners, feats, pool_rows = d_ref.shape
    rows = a_ref.shape[2]
    me = lax.axis_index("tok")
    for g, piece, at in sources(pieces):
        d_ref[g] = piece[at, :feats]
    for g in range(owners):
        spread = lax.dot_general(
            d_ref[g], hot_of(map_ref[g][:blocks], pool_rows), NN, preferred_element_type=F32
        ).astype(BF16)
        for n in range(blocks):
            a_ref[g * blocks + n] = spread[:, n * rows : (n + 1) * rows]
    done = run_sections(a_ref, b_ref, mix_ref, section_bits, True)
    for o in range(4):
        outs[o][...] = done[pl.ds((me // 2 ^ o) * 2 * blocks, 2 * blocks)]


def relay_kernel(came_ref, *refs):
    refs[-1][...] = came_ref[...]


def early_kernel(w_ref, own_ref, came_ref, out_ref):
    outs_tp = own_ref.shape[1]
    place = lax.axis_index("tp")
    total = None
    for o, cot in ((0, own_ref), (2, came_ref)):
        at = pl.multiple_of((place ^ o) * outs_tp, outs_tp)
        part = lax.dot_general(
            cot[...], w_ref[:, pl.ds(at, outs_tp)], NT, preferred_element_type=F32
        )
        total = part if total is None else total + part
    out_ref[...] = total


def cotangent_kernel(w_ref, map_ref, pooled_ref, early_ref, *refs):
    cots, outs_ref, (send_ref, turned_ref) = refs[:4], refs[4:8], refs[8:]
    owners, feats, pool_rows = pooled_ref.shape
    outs_tp = cots[0].shape[1]
    outs = send_ref.shape[1] // 4
    place, me = lax.axis_index("tp"), lax.axis_index("tok")
    other = pl.multiple_of((1 - me % 2) * outs, outs)
    total = early_ref[...]
    for o in (1, 3):
        at = pl.multiple_of((place ^ o) * outs_tp, outs_tp)
        total = total + lax.dot_general(
            cots[o][...], w_ref[:, pl.ds(at, outs_tp)], NT, preferred_element_type=F32
        )
    counts = jnp.zeros((pool_rows, 1), F32)
    maps = lax.rem(map_ref[...], jnp.int32(pool_rows))
    for n in range(maps.shape[0]):
        ids = lax.broadcasted_iota(jnp.int32, (pool_rows, maps.shape[1]), 0)
        hits = (maps[n : n + 1] == ids).astype(F32)
        counts = counts + jnp.sum(hits, axis=1, keepdims=True)
    turned = (total / counts).T.astype(BF16)
    for g in range(owners):
        turned_ref[g] = turned[g * feats : (g + 1) * feats]
    for o in range(4):
        for core in range(2):
            g = (me // 2 ^ o) * 2 + core
            outs_ref[o][core, :feats, :] = turned_ref[g]
            outs_ref[o][core, feats:, :] = pooled_ref[g]
    for o in range(4):
        send_ref[:, o * outs : (o + 1) * outs] = cots[o][:, pl.ds(other, outs)]


def project_kernel(w_ref, came_ref, *refs):
    cots, pieces, (kept_ref, last_ref, sent_ref, held_ref, gone_ref) = refs[:4], refs[4:12], refs[12:17]
    share_ref, part_ref, pool_ref, sems = refs[17:]
    shares = [kept_ref, sent_ref.at[0], last_ref, sent_ref.at[1]]
    feats, pool_rows = pieces[0].shape[1] // 2, pieces[0].shape[2]
    outs_tp = cots[0].shape[1]
    outs = came_ref.shape[1] // 4
    place, me = lax.axis_index("tp"), lax.axis_index("tok")
    copies = []

    def send(source, target):
        copies.append(pltpu.make_async_copy(source, target, sems.at[len(copies)]))
        copies[-1].start()

    mine = pl.multiple_of((me % 2) * outs, outs)
    for g, piece, at in sources(pieces):
        pool_ref[g, :, :pool_rows] = piece[at, feats:, :]
        pool_ref[g, :, pool_rows:] = piece[1 - at, feats:, :]
    turned = jnp.concatenate([pool_ref[g] for g in range(len(pieces))], axis=0)
    pooled = turned[:, :pool_rows].T
    for o in (3, 1, 2, 0):
        at = pl.multiple_of((place ^ o) * outs_tp, outs_tp)
        share_ref[o] = lax.dot_general(
            pooled, w_ref[:, pl.ds(at, outs_tp)], NN, preferred_element_type=F32
        ).astype(BF16)
        send(share_ref.at[o], shares[o])
    for o in range(4):
        own = cots[o][:, pl.ds(mine, outs)]
        cot = jnp.concatenate(
            [own, came_ref[:, o * outs : (o + 1) * outs]], axis=0
        )
        part_ref[place ^ o] = lax.dot_general(
            turned, cot, NN, preferred_element_type=F32
        ).astype(BF16)
    for o in (1, 3, 0, 2):
        send(part_ref.at[(me // 2) ^ o], (gone_ref if o % 2 else held_ref).at[o // 2])
    for copy in copies:
        copy.wait()


def fold_shares_kernel(kept_ref, got_ref, share_ref):
    share_ref[...] = (kept_ref[...].astype(F32) + got_ref[1].astype(F32)).astype(BF16)


def fold_parts_kernel(held_ref, came_ref, part_ref):
    part_ref[...] = (held_ref[1].astype(F32) + came_ref[1].astype(F32)).astype(BF16)


def arrive_kernel(kept_ref, got_ref, share_ref, part_ref, projected_ref, part_out):
    total = kept_ref[...].astype(F32) + got_ref[0].astype(F32) + share_ref[...].astype(F32)
    projected_ref[...] = total.astype(BF16)
    part_out[...] = part_ref[...]


def finish_kernel(scale, *refs):
    pieces, (projected_ref, held_ref, came_ref, part_ref) = refs[:6], refs[6:10]
    tokens_out, projected_out, grad_out, all_ref, tokens_ref, grad_ref, sems = refs[10:]
    blocks, feats, rows = pieces[0].shape[0] // 2, *pieces[0].shape[1:]
    copies = []

    def send(source, target):
        copies.append(pltpu.make_async_copy(source, target, sems.at[len(copies)]))
        copies[-1].start()

    send(projected_ref, projected_out)
    total = held_ref[0].astype(F32) + came_ref[0].astype(F32) + part_ref[...].astype(F32)
    grad_ref[...] = total.T * scale
    send(grad_ref, grad_out)
    for g, piece, at in sources(pieces):
        lanes = pl.ds(pl.multiple_of(g * feats, feats), feats)
        all_ref[:, lanes, :] = piece[pl.ds(at * blocks, blocks)]
    for n in range(blocks):
        tokens_ref[n] = all_ref[n].T
        send(tokens_ref.at[n], tokens_out.at[n])
    for copy in copies:
        copy.wait()


def call(kernel, operands, out_shape, scratch, name, cost=0, out_space=pltpu.VMEM, in_space=pltpu.VMEM):
    several = isinstance(out_shape, (list, tuple))
    into = pl.BlockSpec(memory_space=in_space)
    if in_space == pltpu.HBM:
        operands = [pltpu.with_memory_space_constraint(a, pltpu.HBM) for a in operands]
    spaces = out_space if isinstance(out_space, tuple) else (out_space,) * (len(out_shape) if several else 1)
    out = [pl.BlockSpec(memory_space=space) for space in spaces]
    return pl.pallas_call(
        kernel,
        out_shape=out_shape,
        in_specs=[into] * len(operands),
        out_specs=out if several else out[0],
        scratch_shapes=scratch,
        compiler_params=pltpu.CompilerParams(vmem_limit_bytes=VMEM_LIMIT),
        cost_estimate=pl.CostEstimate(flops=cost, bytes_accessed=0, transcendentals=0),
        name=name,
    )(*operands)


def struct(*shape, dtype=BF16):
    return jax.ShapeDtypeStruct(shape, dtype)


def in_hbm(*shape, dtype=BF16):
    return pltpu.HBM(shape, dtype)


def swap(piece, axis, offset):
    size = lax.axis_size(axis)
    return lax.ppermute(piece, axis, [(i, i ^ offset) for i in range(size)])


def exchange(pieces, halves=False):
    came = [pieces[0]] + [swap(pieces[o], "tok", 2 * o) for o in (1, 2, 3)]
    if not halves:
        return came + [swap(piece, "tok", 1) for piece in came]
    count, *rest = pieces[0].shape
    others = call(gather_kernel, came[:3], struct(3, count // 2, *rest), [], "gather")
    return came + [swap(others, "tok", 1), swap(came[3], "tok", 1)]


def shards(tokens, mix_weights, proj_weight, pool_map, out_cot):
    toks, feats_tp = tokens.shape
    section_count, rows = mix_weights.shape[0], mix_weights.shape[-1]
    owners, groups = lax.axis_size("tok"), lax.axis_size("tp")
    pool_rows, outs_tp = out_cot.shape
    outs = outs_tp * groups // owners
    feats = feats_tp // owners
    blocks = toks // rows
    if feats % 16 or outs % 128 or owners != 8 or groups != 4 or pool_rows > 256 or blocks > TAIL:
        return general_shards(tokens, mix_weights, proj_weight, pool_map, out_cot)
    all_bits = (owners * blocks).bit_length() - 1
    section_bits = [section_id % all_bits for section_id in range(section_count)]
    fields = [pltpu.VMEM((owners * blocks, feats, rows), BF16)] * 2

    across = swap(out_cot, "tp", 2)
    beside = swap(out_cot, "tp", 1)
    onward = call(relay_kernel, (across, beside), struct(pool_rows, outs_tp), [], "relay", RELAY)
    cots = [out_cot, beside, across, swap(onward, "tp", 1)]
    maps = pool_map.reshape(blocks, rows)
    height = blocks * feats + TAIL
    packed = call(
        functools.partial(pack_kernel, pool_rows),
        (tokens.reshape(blocks, rows, feats_tp), maps),
        [struct(2, height, rows)] * 4,
        [
            pltpu.VMEM((blocks, rows, feats_tp), BF16),
            pltpu.VMEM((blocks, rows), jnp.int32),
            pltpu.VMEM((owners, height, rows), BF16),
            pltpu.SemaphoreType.DMA((blocks + 1,)),
        ],
        "pack",
        in_space=pltpu.HBM,
    )
    packed = exchange(packed, True)
    early = call(
        early_kernel,
        (proj_weight, out_cot, across),
        struct(pool_rows, feats_tp, dtype=F32),
        [],
        "early_cotangent",
    )
    pooled, map_rows = call(
        functools.partial(forward_kernel, section_bits, blocks),
        (mix_weights, *packed),
        [struct(owners, feats, pool_rows), struct(owners, TAIL, rows)],
        fields,
        "forward_mix",
    )
    *both, half = call(
        cotangent_kernel,
        (proj_weight, maps, pooled, early, *cots),
        [struct(2, 2 * feats, pool_rows)] * 4 + [struct(pool_rows, groups * outs)],
        [pltpu.VMEM((owners, feats, pool_rows), BF16)],
        "cotangent",
    )
    half = swap(half, "tok", 1)
    both = exchange(both)

    kept, passed, sent, held, gone = call(
        project_kernel,
        (proj_weight, half, *cots, *both),
        [in_hbm(pool_rows, outs_tp)] * 2
        + [in_hbm(2, pool_rows, outs_tp)]
        + [in_hbm(2, feats_tp, outs)] * 2,
        [
            pltpu.VMEM((4, pool_rows, outs_tp), BF16),
            pltpu.VMEM((4, feats_tp, outs), BF16),
            pltpu.VMEM((owners, feats, 2 * pool_rows), BF16),
            pltpu.SemaphoreType.DMA((8,)),
        ],
        "project",
        out_space=pltpu.HBM,
    )
    sent, gone = swap(sent, "tp", 1), swap(gone, "tok", 2)
    share = call(
        fold_shares_kernel,
        (passed, sent),
        struct(pool_rows, outs_tp),
        [],
        "fold_shares",
        0,
    )
    part = call(
        fold_parts_kernel, (held, gone), struct(feats_tp, outs), [], "fold_parts", 0
    )
    share = swap(share, "tp", 2)
    part = swap(part, "tok", 4)
    projected, part = call(
        arrive_kernel,
        (kept, sent, share, part),
        [struct(pool_rows, outs_tp), struct(feats_tp, outs)],
        [],
        "arrive",
        SUMS,
    )

    grad = call(
        functools.partial(backward_kernel, section_bits, blocks),
        (mix_weights, map_rows, *both),
        [struct(2 * blocks, feats, rows)] * 4,
        fields + [pltpu.VMEM((owners, feats, pool_rows), BF16)],
        "backward_mix",
    )
    token_grad, projected, proj_grad = call(
        functools.partial(finish_kernel, 1.0 / math.sqrt(pool_rows * owners)),
        (*exchange(grad, True), projected, held, gone, part),
        [
            in_hbm(blocks, rows, feats_tp),
            in_hbm(pool_rows, outs_tp),
            in_hbm(outs, feats_tp, dtype=F32),
        ],
        [
            pltpu.VMEM((blocks, feats_tp, rows), BF16),
            pltpu.VMEM((blocks, rows, feats_tp), BF16),
            pltpu.VMEM((outs, feats_tp), F32),
            pltpu.SemaphoreType.DMA((blocks + 2,)),
        ],
        "finish",
        out_space=pltpu.HBM,
    )
    token_grad = token_grad.reshape(toks, feats_tp)
    return (projected, token_grad, proj_grad)


def solution(mesh):
    in_specs = (P("tok", "tp"), P(), P("tp", None), P("tok"), P("tok", "tp"))
    out_specs = (P("tok", "tp"), P("tok", "tp"), P("tok", "tp"))
    return jax.shard_map(shards, mesh=mesh, in_specs=in_specs, out_specs=out_specs, check_vma=False)
```

```python
import functools
import math

import jax
import jax.numpy as jnp
from jax import lax
from jax.experimental import pallas as pl
from jax.experimental.pallas import tpu as pltpu
from jax.sharding import PartitionSpec as P

F32 = jnp.float32
BF16 = jnp.bfloat16
VMEM_LIMIT = 40 * 1024 * 1024
NT = (((1,), (1,)), ((), ()))
NN = (((1,), (0,)), ((), ()))
TAIL = 16
RELAY = 5_000_000_000
SUMS = 1_000_000_000


def contract(matrix, operand, backward):
    pattern = "ji,...j->...i" if backward else "ij,...j->...i"
    return jnp.einsum(pattern, matrix, operand, preferred_element_type=jnp.float32)


def local_section(field_now, section_mats, bit_index, backward, block_axis):
    full_shape = field_now.shape
    nblocks = full_shape[block_axis]
    split_shape = (
        full_shape[:block_axis]
        + (nblocks >> bit_index + 1, 2, 1 << bit_index)
        + full_shape[block_axis + 1 :]
    )
    paired = field_now.reshape(split_shape)
    lower_half = lax.index_in_dim(paired, 0, block_axis + 1, keepdims=False)
    upper_half = lax.index_in_dim(paired, 1, block_axis + 1, keepdims=False)
    if backward:
        new_lower = contract(section_mats[0, 0], lower_half, True) + contract(
            section_mats[1, 0], upper_half, True
        )
        new_upper = contract(section_mats[0, 1], lower_half, True) + contract(
            section_mats[1, 1], upper_half, True
        )
    else:
        new_lower = contract(section_mats[0, 0], lower_half, False) + contract(
            section_mats[0, 1], upper_half, False
        )
        new_upper = contract(section_mats[1, 0], lower_half, False) + contract(
            section_mats[1, 1], upper_half, False
        )
    joined = jnp.stack(
        [new_lower.astype(jnp.bfloat16), new_upper.astype(jnp.bfloat16)], axis=block_axis + 1
    )
    return joined.reshape(full_shape)


def mix_tokens(source, mix_weights, section_bits, backward):
    block_rows = mix_weights.shape[-1]
    section_order = list(range(len(section_bits)))
    if backward:
        section_order = section_order[::-1]
    columns = lax.all_to_all(source.T, "tok", split_axis=0, concat_axis=1, tiled=True)
    feat_rows, all_tokens = columns.shape
    field_now = columns.reshape(feat_rows, all_tokens // block_rows, block_rows)
    for section_id in section_order:
        field_now = local_section(
            field_now, mix_weights[section_id], section_bits[section_id], backward, 1
        )
    back_rows = lax.all_to_all(
        field_now.reshape(feat_rows, all_tokens), "tok", split_axis=1, concat_axis=0, tiled=True
    )
    return back_rows.T


def general_shards(tokens, mix_weights, proj_weight, pool_map, out_cot):
    tok_rows = tokens.shape[0]
    block_rows = mix_weights.shape[-1]
    section_count = mix_weights.shape[0]
    local_blocks = tok_rows // block_rows
    local_bits = local_blocks.bit_length() - 1
    tok_devices = lax.axis_size("tok")
    all_bits = local_bits + tok_devices.bit_length() - 1
    section_bits = [section_id % all_bits for section_id in range(section_count)]
    mixed = mix_tokens(tokens, mix_weights, section_bits, False)
    pool_rows = out_cot.shape[0]
    local_map = pool_map - lax.axis_index("tok") * pool_rows
    membership = (local_map[None, :] == jnp.arange(pool_rows, dtype=jnp.int32)[:, None]).astype(
        jnp.bfloat16
    )
    counts = jnp.sum(membership.astype(jnp.float32), axis=1)
    group_sums = jnp.dot(membership, mixed, preferred_element_type=jnp.float32)
    pooled = (group_sums / counts[:, None]).astype(jnp.bfloat16)
    proj_share = lax.psum_scatter(
        lax.dot_general(
            proj_weight, pooled, (((0,), (1,)), ((), ())), preferred_element_type=jnp.float32
        ).astype(jnp.bfloat16),
        "tp",
        scatter_dimension=0,
        tiled=True,
    ).astype(jnp.float32)
    projected = proj_share.T.astype(jnp.bfloat16)
    cot_full = lax.all_gather(out_cot, "tp", axis=1, tiled=True)
    d_pooled = lax.dot_general(
        cot_full, proj_weight, (((1,), (1,)), ((), ())), preferred_element_type=jnp.float32
    )
    back_rows = jnp.take(d_pooled / counts[:, None], local_map, axis=0).astype(jnp.bfloat16)
    token_grad = mix_tokens(back_rows, mix_weights, section_bits, True)
    grad_share = lax.psum_scatter(
        lax.dot_general(
            cot_full, pooled, (((0,), (0,)), ((), ())), preferred_element_type=jnp.float32
        ),
        "tok",
        scatter_dimension=0,
        tiled=True,
    )
    grad_scale = 1.0 / math.sqrt(pool_rows * tok_devices)
    proj_grad = grad_share * grad_scale
    return (projected, token_grad, proj_grad)


def one_hot(map_row, pool_rows):
    ids = lax.broadcasted_iota(jnp.int32, (pool_rows, map_row.shape[-1]), 0)
    return (map_row == ids).astype(BF16)


def run_sections(field, other, mix_ref, section_bits, backward):
    blocks, feats, rows = field.shape
    order = list(enumerate(section_bits))
    for section_id, bit in order[::-1] if backward else order:
        m = [[mix_ref[section_id, a, b] for b in range(2)] for a in range(2)]
        full = jnp.concatenate(
            [jnp.concatenate(m[0], axis=1), jnp.concatenate(m[1], axis=1)], axis=0
        )
        lows = [b for b in range(blocks) if not (b >> bit) & 1]
        step = max(1, 512 // feats)
        for at in range(0, len(lows), step):
            part = lows[at : at + step]
            low = jnp.concatenate([field[b] for b in part], axis=0)
            high = jnp.concatenate([field[b + (1 << bit)] for b in part], axis=0)
            pair = jnp.concatenate([low, high], axis=1)
            out = lax.dot_general(
                pair, full, NN if backward else NT, preferred_element_type=F32
            ).astype(BF16)
            for n, b in enumerate(part):
                other[b] = out[n * feats : (n + 1) * feats, :rows]
                other[b + (1 << bit)] = out[n * feats : (n + 1) * feats, rows:]
        field, other = other, field
    return field


def pack_kernel(pool_rows, tokens_ref, map_ref, *refs):
    outs, (held_ref, maps_ref, packed_ref, sems) = refs[:4], refs[4:]
    blocks, rows = map_ref.shape
    owners = packed_ref.shape[0]
    feats = tokens_ref.shape[2] // owners
    loads = [
        pltpu.make_async_copy(tokens_ref.at[n], held_ref.at[n], sems.at[n]) for n in range(blocks)
    ]
    loads.append(pltpu.make_async_copy(map_ref, maps_ref, sems.at[blocks]))
    for load in loads:
        load.start()
    loads[blocks].wait()
    maps = lax.rem(maps_ref[...], jnp.int32(pool_rows)).astype(F32).astype(BF16)
    tail = jnp.concatenate([maps, jnp.zeros((TAIL - blocks, rows), BF16)], axis=0)
    for g in range(owners):
        packed_ref[g, blocks * feats :, :] = tail
    for n in range(blocks):
        loads[n].wait()
        turned = held_ref[n].T
        for g in range(owners):
            packed_ref[g, n * feats : (n + 1) * feats, :] = turned[g * feats : (g + 1) * feats]
    chip = lax.axis_index("tok") // 2
    for o in range(4):
        outs[o][...] = packed_ref[pl.ds((chip ^ o) * 2, 2)]


def hot_of(maps, pool_rows):
    maps = maps.astype(F32).astype(jnp.int32)
    return jnp.concatenate(
        [one_hot(maps[n : n + 1], pool_rows) for n in range(maps.shape[0])], axis=1
    )


def sources(pieces):
    me = lax.axis_index("tok")
    if len(pieces) == 8:
        for k, piece in enumerate(pieces):
            yield me ^ (2 * (k % 4) + k // 4), piece, me % 2
        return
    for k, piece in enumerate(pieces[:4]):
        yield me ^ (2 * k), piece, me % 2
    for k in range(3):
        yield me ^ (2 * k + 1), pieces[4].at[k], 0
    yield me ^ 7, pieces[5], me % 2


def gather_kernel(*refs):
    *pieces, out_ref = refs
    count = out_ref.shape[1]
    other = 1 - lax.axis_index("tok") % 2
    for k, piece in enumerate(pieces):
        out_ref[k] = piece[pl.ds(other * count, count)]


def forward_kernel(section_bits, blocks, mix_ref, *refs):
    pieces, (out_ref, map_ref, a_ref, b_ref) = refs[:6], refs[6:]
    owners, feats, pool_rows = out_ref.shape
    rows = a_ref.shape[2]
    for g, piece, at in sources(pieces):
        map_ref[g] = piece[at, blocks * feats :, :]
        for n in range(blocks):
            a_ref[g * blocks + n] = piece[at, n * feats : (n + 1) * feats, :]
    done = run_sections(a_ref, b_ref, mix_ref, section_bits, False)
    ones = jnp.ones((16, blocks * rows), BF16)
    for g in range(owners):
        mine = jnp.concatenate([done[g * blocks + n] for n in range(blocks)], axis=1)
        sums = lax.dot_general(
            jnp.concatenate([mine, ones], axis=0),
            hot_of(map_ref[g][:blocks], pool_rows),
            NT,
            preferred_element_type=F32,
        )
        out_ref[g] = (sums[:feats] / sums[feats : feats + 1]).astype(BF16)


def backward_kernel(section_bits, blocks, mix_ref, map_ref, *refs):
    pieces, outs, (a_ref, b_ref, d_ref) = refs[:8], refs[8:12], refs[12:]
    owners, feats, pool_rows = d_ref.shape
    rows = a_ref.shape[2]
    me = lax.axis_index("tok")
    for g, piece, at in sources(pieces):
        d_ref[g] = piece[at, :feats]
    for g in range(owners):
        spread = lax.dot_general(
            d_ref[g], hot_of(map_ref[g][:blocks], pool_rows), NN, preferred_element_type=F32
        ).astype(BF16)
        for n in range(blocks):
            a_ref[g * blocks + n] = spread[:, n * rows : (n + 1) * rows]
    done = run_sections(a_ref, b_ref, mix_ref, section_bits, True)
    for o in range(4):
        outs[o][...] = done[pl.ds((me // 2 ^ o) * 2 * blocks, 2 * blocks)]


def relay_kernel(came_ref, *refs):
    refs[-1][...] = came_ref[...]


def early_kernel(w_ref, own_ref, came_ref, out_ref):
    outs_tp = own_ref.shape[1]
    place = lax.axis_index("tp")
    total = None
    for o, cot in ((0, own_ref), (2, came_ref)):
        at = pl.multiple_of((place ^ o) * outs_tp, outs_tp)
        part = lax.dot_general(
            cot[...], w_ref[:, pl.ds(at, outs_tp)], NT, preferred_element_type=F32
        )
        total = part if total is None else total + part
    out_ref[...] = total


def cotangent_kernel(w_ref, map_ref, pooled_ref, early_ref, *refs):
    cots, outs_ref, (send_ref, turned_ref) = refs[:4], refs[4:8], refs[8:]
    owners, feats, pool_rows = pooled_ref.shape
    outs_tp = cots[0].shape[1]
    outs = send_ref.shape[1] // 4
    place, me = lax.axis_index("tp"), lax.axis_index("tok")
    other = pl.multiple_of((1 - me % 2) * outs, outs)
    total = early_ref[...]
    for o in (1, 3):
        at = pl.multiple_of((place ^ o) * outs_tp, outs_tp)
        total = total + lax.dot_general(
            cots[o][...], w_ref[:, pl.ds(at, outs_tp)], NT, preferred_element_type=F32
        )
    counts = jnp.zeros((pool_rows, 1), F32)
    maps = lax.rem(map_ref[...], jnp.int32(pool_rows))
    for n in range(maps.shape[0]):
        ids = lax.broadcasted_iota(jnp.int32, (pool_rows, maps.shape[1]), 0)
        hits = (maps[n : n + 1] == ids).astype(F32)
        counts = counts + jnp.sum(hits, axis=1, keepdims=True)
    turned = (total / counts).T.astype(BF16)
    for g in range(owners):
        turned_ref[g] = turned[g * feats : (g + 1) * feats]
    for o in range(4):
        for core in range(2):
            g = (me // 2 ^ o) * 2 + core
            outs_ref[o][core, :feats, :] = turned_ref[g]
            outs_ref[o][core, feats:, :] = pooled_ref[g]
    for o in range(4):
        send_ref[:, o * outs : (o + 1) * outs] = cots[o][:, pl.ds(other, outs)]


def project_kernel(w_ref, *refs):
    pieces, (kept_ref, passed_ref, sent_ref, share_ref, pool_ref, sems) = refs[:8], refs[8:]
    feats = pieces[0].shape[1] // 2
    outs_tp = share_ref.shape[2]
    place = lax.axis_index("tp")
    targets = [kept_ref, sent_ref.at[0], passed_ref, sent_ref.at[1]]
    for g, piece, at in sources(pieces):
        pool_ref[g] = piece[at, feats:, :]
    pooled = jnp.concatenate([pool_ref[g] for g in range(len(pieces))], axis=0).T
    copies = []
    for o in (3, 1, 2, 0):
        at = pl.multiple_of((place ^ o) * outs_tp, outs_tp)
        share_ref[o] = lax.dot_general(
            pooled, w_ref[:, pl.ds(at, outs_tp)], NN, preferred_element_type=F32
        ).astype(BF16)
        copies.append(pltpu.make_async_copy(share_ref.at[o], targets[o], sems.at[o]))
        copies[-1].start()
    for copy in copies:
        copy.wait()


def gradient_kernel(came_ref, *refs):
    cots, pieces, (held_ref, gone_ref, part_ref, pool_ref, sems) = refs[:4], refs[4:12], refs[-5:]
    feats, pool_rows = pieces[0].shape[1] // 2, pieces[0].shape[2]
    outs = came_ref.shape[1] // 4
    place, me = lax.axis_index("tp"), lax.axis_index("tok")
    mine = pl.multiple_of((me % 2) * outs, outs)
    for g, piece, at in sources(pieces):
        pool_ref[g, :, :pool_rows] = piece[at, feats:, :]
        pool_ref[g, :, pool_rows:] = piece[1 - at, feats:, :]
    turned = jnp.concatenate([pool_ref[g] for g in range(len(pieces))], axis=0)
    for o in range(4):
        own = cots[o][:, pl.ds(mine, outs)]
        cot = jnp.concatenate([own, came_ref[:, o * outs : (o + 1) * outs]], axis=0)
        part_ref[place ^ o] = lax.dot_general(
            turned, cot, NN, preferred_element_type=F32
        ).astype(BF16)
    copies = []
    for o in (1, 3, 0, 2):
        target = (gone_ref if o % 2 else held_ref).at[o // 2]
        copies.append(pltpu.make_async_copy(part_ref.at[(me // 2) ^ o], target, sems.at[o]))
        copies[-1].start()
    for copy in copies:
        copy.wait()


def fold_shares_kernel(kept_ref, got_ref, share_ref):
    share_ref[...] = (kept_ref[...].astype(F32) + got_ref[1].astype(F32)).astype(BF16)


def fold_parts_kernel(held_ref, came_ref, part_ref):
    part_ref[...] = (held_ref[1].astype(F32) + came_ref[1].astype(F32)).astype(BF16)


def arrive_kernel(kept_ref, got_ref, share_ref, part_ref, projected_ref, part_out):
    total = kept_ref[...].astype(F32) + got_ref[0].astype(F32) + share_ref[...].astype(F32)
    projected_ref[...] = total.astype(BF16)
    part_out[...] = part_ref[...]


def finish_kernel(scale, *refs):
    pieces, (projected_ref, held_ref, came_ref, part_ref) = refs[:6], refs[6:10]
    tokens_out, projected_out, grad_out, all_ref, tokens_ref, grad_ref, sems = refs[10:]
    blocks, feats, rows = pieces[0].shape[0] // 2, *pieces[0].shape[1:]
    copies = []

    def send(source, target):
        copies.append(pltpu.make_async_copy(source, target, sems.at[len(copies)]))
        copies[-1].start()

    send(projected_ref, projected_out)
    total = held_ref[0].astype(F32) + came_ref[0].astype(F32) + part_ref[...].astype(F32)
    grad_ref[...] = total.T * scale
    send(grad_ref, grad_out)
    for g, piece, at in sources(pieces):
        lanes = pl.ds(pl.multiple_of(g * feats, feats), feats)
        all_ref[:, lanes, :] = piece[pl.ds(at * blocks, blocks)]
    for n in range(blocks):
        tokens_ref[n] = all_ref[n].T
        send(tokens_ref.at[n], tokens_out.at[n])
    for copy in copies:
        copy.wait()


def call(kernel, operands, out_shape, scratch, name, cost=0, out_space=pltpu.VMEM, in_space=pltpu.VMEM):
    several = isinstance(out_shape, (list, tuple))
    into = pl.BlockSpec(memory_space=in_space)
    if in_space == pltpu.HBM:
        operands = [pltpu.with_memory_space_constraint(a, pltpu.HBM) for a in operands]
    spaces = out_space if isinstance(out_space, tuple) else (out_space,) * (len(out_shape) if several else 1)
    out = [pl.BlockSpec(memory_space=space) for space in spaces]
    return pl.pallas_call(
        kernel,
        out_shape=out_shape,
        in_specs=[into] * len(operands),
        out_specs=out if several else out[0],
        scratch_shapes=scratch,
        compiler_params=pltpu.CompilerParams(vmem_limit_bytes=VMEM_LIMIT),
        cost_estimate=pl.CostEstimate(flops=cost, bytes_accessed=0, transcendentals=0),
        name=name,
    )(*operands)


def struct(*shape, dtype=BF16):
    return jax.ShapeDtypeStruct(shape, dtype)


def in_hbm(*shape, dtype=BF16):
    return pltpu.HBM(shape, dtype)


def swap(piece, axis, offset):
    size = lax.axis_size(axis)
    return lax.ppermute(piece, axis, [(i, i ^ offset) for i in range(size)])


def exchange(pieces, halves=False):
    came = [pieces[0]] + [swap(pieces[o], "tok", 2 * o) for o in (1, 2, 3)]
    if not halves:
        return came + [swap(piece, "tok", 1) for piece in came]
    count, *rest = pieces[0].shape
    others = call(gather_kernel, came[:3], struct(3, count // 2, *rest), [], "gather")
    return came + [swap(others, "tok", 1), swap(came[3], "tok", 1)]


def shards(tokens, mix_weights, proj_weight, pool_map, out_cot):
    toks, feats_tp = tokens.shape
    section_count, rows = mix_weights.shape[0], mix_weights.shape[-1]
    owners, groups = lax.axis_size("tok"), lax.axis_size("tp")
    pool_rows, outs_tp = out_cot.shape
    outs = outs_tp * groups // owners
    feats = feats_tp // owners
    blocks = toks // rows
    if feats % 16 or outs % 128 or owners != 8 or groups != 4 or pool_rows > 256 or blocks > TAIL:
        return general_shards(tokens, mix_weights, proj_weight, pool_map, out_cot)
    all_bits = (owners * blocks).bit_length() - 1
    section_bits = [section_id % all_bits for section_id in range(section_count)]
    fields = [pltpu.VMEM((owners * blocks, feats, rows), BF16)] * 2

    across = swap(out_cot, "tp", 2)
    beside = swap(out_cot, "tp", 1)
    onward = call(relay_kernel, (across, beside), struct(pool_rows, outs_tp), [], "relay", RELAY)
    cots = [out_cot, beside, across, swap(onward, "tp", 1)]
    maps = pool_map.reshape(blocks, rows)
    height = blocks * feats + TAIL
    packed = call(
        functools.partial(pack_kernel, pool_rows),
        (tokens.reshape(blocks, rows, feats_tp), maps),
        [struct(2, height, rows)] * 4,
        [
            pltpu.VMEM((blocks, rows, feats_tp), BF16),
            pltpu.VMEM((blocks, rows), jnp.int32),
            pltpu.VMEM((owners, height, rows), BF16),
            pltpu.SemaphoreType.DMA((blocks + 1,)),
        ],
        "pack",
        in_space=pltpu.HBM,
    )
    packed = exchange(packed, True)
    pooled, map_rows = call(
        functools.partial(forward_kernel, section_bits, blocks),
        (mix_weights, *packed),
        [struct(owners, feats, pool_rows), struct(owners, TAIL, rows)],
        fields,
        "forward_mix",
    )
    pooled, later = lax.optimization_barrier((pooled, across))
    early = call(
        early_kernel,
        (proj_weight, out_cot, later),
        struct(pool_rows, feats_tp, dtype=F32),
        [],
        "early_cotangent",
    )
    *both, half = call(
        cotangent_kernel,
        (proj_weight, maps, pooled, early, *cots),
        [struct(2, 2 * feats, pool_rows)] * 4 + [struct(pool_rows, groups * outs)],
        [pltpu.VMEM((owners, feats, pool_rows), BF16)],
        "cotangent",
    )
    half = swap(half, "tok", 1)
    both = exchange(both)

    kept, passed, sent = call(
        project_kernel,
        (proj_weight, *both),
        [in_hbm(pool_rows, outs_tp)] * 2 + [in_hbm(2, pool_rows, outs_tp)],
        [
            pltpu.VMEM((4, pool_rows, outs_tp), BF16),
            pltpu.VMEM((owners, feats, pool_rows), BF16),
            pltpu.SemaphoreType.DMA((4,)),
        ],
        "project",
        out_space=pltpu.HBM,
    )
    half, passed = lax.optimization_barrier((half, passed))
    held, gone = call(
        gradient_kernel,
        (half, *cots, *both),
        [in_hbm(2, feats_tp, outs)] * 2,
        [
            pltpu.VMEM((4, feats_tp, outs), BF16),
            pltpu.VMEM((owners, feats, 2 * pool_rows), BF16),
            pltpu.SemaphoreType.DMA((4,)),
        ],
        "projector_gradient",
        out_space=pltpu.HBM,
    )
    sent, gone = swap(sent, "tp", 1), swap(gone, "tok", 2)
    share = call(
        fold_shares_kernel,
        (passed, sent),
        struct(pool_rows, outs_tp),
        [],
        "fold_shares",
        0,
    )
    part = call(
        fold_parts_kernel, (held, gone), struct(feats_tp, outs), [], "fold_parts", 0
    )
    share = swap(share, "tp", 2)
    part = swap(part, "tok", 4)
    projected, part = call(
        arrive_kernel,
        (kept, sent, share, part),
        [struct(pool_rows, outs_tp), struct(feats_tp, outs)],
        [],
        "arrive",
        SUMS,
    )

    grad = call(
        functools.partial(backward_kernel, section_bits, blocks),
        (mix_weights, map_rows, *both),
        [struct(2 * blocks, feats, rows)] * 4,
        fields + [pltpu.VMEM((owners, feats, pool_rows), BF16)],
        "backward_mix",
    )
    token_grad, projected, proj_grad = call(
        functools.partial(finish_kernel, 1.0 / math.sqrt(pool_rows * owners)),
        (*exchange(grad, True), projected, held, gone, part),
        [
            in_hbm(blocks, rows, feats_tp),
            in_hbm(pool_rows, outs_tp),
            in_hbm(outs, feats_tp, dtype=F32),
        ],
        [
            pltpu.VMEM((blocks, feats_tp, rows), BF16),
            pltpu.VMEM((blocks, rows, feats_tp), BF16),
            pltpu.VMEM((outs, feats_tp), F32),
            pltpu.SemaphoreType.DMA((blocks + 2,)),
        ],
        "finish",
        out_space=pltpu.HBM,
    )
    token_grad = token_grad.reshape(toks, feats_tp)
    return (projected, token_grad, proj_grad)


def solution(mesh):
    in_specs = (P("tok", "tp"), P(), P("tp", None), P("tok"), P("tok", "tp"))
    out_specs = (P("tok", "tp"), P("tok", "tp"), P("tok", "tp"))
    return jax.shard_map(shards, mesh=mesh, in_specs=in_specs, out_specs=out_specs, check_vma=False)
```

```python
import functools
import math

import jax
import jax.numpy as jnp
from jax import lax
from jax.experimental import pallas as pl
from jax.experimental.pallas import tpu as pltpu
from jax.sharding import PartitionSpec as P

F32 = jnp.float32
BF16 = jnp.bfloat16
VMEM_LIMIT = 40 * 1024 * 1024
NT = (((1,), (1,)), ((), ()))
NN = (((1,), (0,)), ((), ()))
TAIL = 16
RELAY = 5_000_000_000
SUMS = 1_000_000_000


def contract(matrix, operand, backward):
    pattern = "ji,...j->...i" if backward else "ij,...j->...i"
    return jnp.einsum(pattern, matrix, operand, preferred_element_type=jnp.float32)


def local_section(field_now, section_mats, bit_index, backward, block_axis):
    full_shape = field_now.shape
    nblocks = full_shape[block_axis]
    split_shape = (
        full_shape[:block_axis]
        + (nblocks >> bit_index + 1, 2, 1 << bit_index)
        + full_shape[block_axis + 1 :]
    )
    paired = field_now.reshape(split_shape)
    lower_half = lax.index_in_dim(paired, 0, block_axis + 1, keepdims=False)
    upper_half = lax.index_in_dim(paired, 1, block_axis + 1, keepdims=False)
    if backward:
        new_lower = contract(section_mats[0, 0], lower_half, True) + contract(
            section_mats[1, 0], upper_half, True
        )
        new_upper = contract(section_mats[0, 1], lower_half, True) + contract(
            section_mats[1, 1], upper_half, True
        )
    else:
        new_lower = contract(section_mats[0, 0], lower_half, False) + contract(
            section_mats[0, 1], upper_half, False
        )
        new_upper = contract(section_mats[1, 0], lower_half, False) + contract(
            section_mats[1, 1], upper_half, False
        )
    joined = jnp.stack(
        [new_lower.astype(jnp.bfloat16), new_upper.astype(jnp.bfloat16)], axis=block_axis + 1
    )
    return joined.reshape(full_shape)


def mix_tokens(source, mix_weights, section_bits, backward):
    block_rows = mix_weights.shape[-1]
    section_order = list(range(len(section_bits)))
    if backward:
        section_order = section_order[::-1]
    columns = lax.all_to_all(source.T, "tok", split_axis=0, concat_axis=1, tiled=True)
    feat_rows, all_tokens = columns.shape
    field_now = columns.reshape(feat_rows, all_tokens // block_rows, block_rows)
    for section_id in section_order:
        field_now = local_section(
            field_now, mix_weights[section_id], section_bits[section_id], backward, 1
        )
    back_rows = lax.all_to_all(
        field_now.reshape(feat_rows, all_tokens), "tok", split_axis=1, concat_axis=0, tiled=True
    )
    return back_rows.T


def general_shards(tokens, mix_weights, proj_weight, pool_map, out_cot):
    tok_rows = tokens.shape[0]
    block_rows = mix_weights.shape[-1]
    section_count = mix_weights.shape[0]
    local_blocks = tok_rows // block_rows
    local_bits = local_blocks.bit_length() - 1
    tok_devices = lax.axis_size("tok")
    all_bits = local_bits + tok_devices.bit_length() - 1
    section_bits = [section_id % all_bits for section_id in range(section_count)]
    mixed = mix_tokens(tokens, mix_weights, section_bits, False)
    pool_rows = out_cot.shape[0]
    local_map = pool_map - lax.axis_index("tok") * pool_rows
    membership = (local_map[None, :] == jnp.arange(pool_rows, dtype=jnp.int32)[:, None]).astype(
        jnp.bfloat16
    )
    counts = jnp.sum(membership.astype(jnp.float32), axis=1)
    group_sums = jnp.dot(membership, mixed, preferred_element_type=jnp.float32)
    pooled = (group_sums / counts[:, None]).astype(jnp.bfloat16)
    proj_share = lax.psum_scatter(
        lax.dot_general(
            proj_weight, pooled, (((0,), (1,)), ((), ())), preferred_element_type=jnp.float32
        ).astype(jnp.bfloat16),
        "tp",
        scatter_dimension=0,
        tiled=True,
    ).astype(jnp.float32)
    projected = proj_share.T.astype(jnp.bfloat16)
    cot_full = lax.all_gather(out_cot, "tp", axis=1, tiled=True)
    d_pooled = lax.dot_general(
        cot_full, proj_weight, (((1,), (1,)), ((), ())), preferred_element_type=jnp.float32
    )
    back_rows = jnp.take(d_pooled / counts[:, None], local_map, axis=0).astype(jnp.bfloat16)
    token_grad = mix_tokens(back_rows, mix_weights, section_bits, True)
    grad_share = lax.psum_scatter(
        lax.dot_general(
            cot_full, pooled, (((0,), (0,)), ((), ())), preferred_element_type=jnp.float32
        ),
        "tok",
        scatter_dimension=0,
        tiled=True,
    )
    grad_scale = 1.0 / math.sqrt(pool_rows * tok_devices)
    proj_grad = grad_share * grad_scale
    return (projected, token_grad, proj_grad)


def one_hot(map_row, pool_rows):
    ids = lax.broadcasted_iota(jnp.int32, (pool_rows, map_row.shape[-1]), 0)
    return (map_row == ids).astype(BF16)


def run_sections(field, other, mix_ref, section_bits, backward):
    blocks, feats, rows = field.shape
    order = list(enumerate(section_bits))
    for section_id, bit in order[::-1] if backward else order:
        m = [[mix_ref[section_id, a, b] for b in range(2)] for a in range(2)]
        full = jnp.concatenate(
            [jnp.concatenate(m[0], axis=1), jnp.concatenate(m[1], axis=1)], axis=0
        )
        lows = [b for b in range(blocks) if not (b >> bit) & 1]
        step = max(1, 512 // feats)
        for at in range(0, len(lows), step):
            part = lows[at : at + step]
            low = jnp.concatenate([field[b] for b in part], axis=0)
            high = jnp.concatenate([field[b + (1 << bit)] for b in part], axis=0)
            pair = jnp.concatenate([low, high], axis=1)
            out = lax.dot_general(
                pair, full, NN if backward else NT, preferred_element_type=F32
            ).astype(BF16)
            for n, b in enumerate(part):
                other[b] = out[n * feats : (n + 1) * feats, :rows]
                other[b + (1 << bit)] = out[n * feats : (n + 1) * feats, rows:]
        field, other = other, field
    return field


def pack_kernel(pool_rows, tokens_ref, map_ref, *refs):
    outs, (held_ref, maps_ref, packed_ref, sems) = refs[:4], refs[4:]
    blocks, rows = map_ref.shape
    owners = packed_ref.shape[0]
    feats = tokens_ref.shape[2] // owners
    loads = [
        pltpu.make_async_copy(tokens_ref.at[n], held_ref.at[n], sems.at[n]) for n in range(blocks)
    ]
    loads.append(pltpu.make_async_copy(map_ref, maps_ref, sems.at[blocks]))
    for load in loads:
        load.start()
    loads[blocks].wait()
    maps = lax.rem(maps_ref[...], jnp.int32(pool_rows)).astype(F32).astype(BF16)
    tail = jnp.concatenate([maps, jnp.zeros((TAIL - blocks, rows), BF16)], axis=0)
    for g in range(owners):
        packed_ref[g, blocks * feats :, :] = tail
    for n in range(blocks):
        loads[n].wait()
        turned = held_ref[n].T
        for g in range(owners):
            packed_ref[g, n * feats : (n + 1) * feats, :] = turned[g * feats : (g + 1) * feats]
    chip = lax.axis_index("tok") // 2
    for o in range(4):
        outs[o][...] = packed_ref[pl.ds((chip ^ o) * 2, 2)]


def hot_of(maps, pool_rows):
    maps = maps.astype(F32).astype(jnp.int32)
    return jnp.concatenate(
        [one_hot(maps[n : n + 1], pool_rows) for n in range(maps.shape[0])], axis=1
    )


def sources(pieces):
    me = lax.axis_index("tok")
    if len(pieces) == 8:
        for k, piece in enumerate(pieces):
            yield me ^ (2 * (k % 4) + k // 4), piece, me % 2
        return
    for k, piece in enumerate(pieces[:4]):
        yield me ^ (2 * k), piece, me % 2
    for k in range(3):
        yield me ^ (2 * k + 1), pieces[4].at[k], 0
    yield me ^ 7, pieces[5], me % 2


def gather_kernel(*refs):
    *pieces, out_ref = refs
    count = out_ref.shape[1]
    other = 1 - lax.axis_index("tok") % 2
    for k, piece in enumerate(pieces):
        out_ref[k] = piece[pl.ds(other * count, count)]


def forward_kernel(section_bits, blocks, mix_ref, *refs):
    pieces, (out_ref, map_ref, a_ref, b_ref) = refs[:6], refs[6:]
    owners, feats, pool_rows = out_ref.shape
    rows = a_ref.shape[2]
    for g, piece, at in sources(pieces):
        map_ref[g] = piece[at, blocks * feats :, :]
        for n in range(blocks):
            a_ref[g * blocks + n] = piece[at, n * feats : (n + 1) * feats, :]
    done = run_sections(a_ref, b_ref, mix_ref, section_bits, False)
    ones = jnp.ones((16, blocks * rows), BF16)
    for g in range(owners):
        mine = jnp.concatenate([done[g * blocks + n] for n in range(blocks)], axis=1)
        sums = lax.dot_general(
            jnp.concatenate([mine, ones], axis=0),
            hot_of(map_ref[g][:blocks], pool_rows),
            NT,
            preferred_element_type=F32,
        )
        out_ref[g] = (sums[:feats] / sums[feats : feats + 1]).astype(BF16)


def backward_kernel(section_bits, blocks, mix_ref, map_ref, *refs):
    pieces, outs, (a_ref, b_ref, d_ref) = refs[:8], refs[8:12], refs[12:]
    owners, feats, pool_rows = d_ref.shape
    rows = a_ref.shape[2]
    me = lax.axis_index("tok")
    for g, piece, at in sources(pieces):
        d_ref[g] = piece[at, :feats]
    for g in range(owners):
        spread = lax.dot_general(
            d_ref[g], hot_of(map_ref[g][:blocks], pool_rows), NN, preferred_element_type=F32
        ).astype(BF16)
        for n in range(blocks):
            a_ref[g * blocks + n] = spread[:, n * rows : (n + 1) * rows]
    done = run_sections(a_ref, b_ref, mix_ref, section_bits, True)
    for o in range(4):
        outs[o][...] = done[pl.ds((me // 2 ^ o) * 2 * blocks, 2 * blocks)]


def relay_kernel(came_ref, *refs):
    refs[-1][...] = came_ref[...]


def early_kernel(w_ref, own_ref, came_ref, out_ref):
    outs_tp = own_ref.shape[1]
    place = lax.axis_index("tp")
    total = None
    for o, cot in ((0, own_ref), (2, came_ref)):
        at = pl.multiple_of((place ^ o) * outs_tp, outs_tp)
        part = lax.dot_general(
            cot[...], w_ref[:, pl.ds(at, outs_tp)], NT, preferred_element_type=F32
        )
        total = part if total is None else total + part
    out_ref[...] = total


def cotangent_kernel(w_ref, map_ref, pooled_ref, early_ref, *refs):
    cots, outs_ref, (send_ref, turned_ref) = refs[:4], refs[4:8], refs[8:]
    owners, feats, pool_rows = pooled_ref.shape
    outs_tp = cots[0].shape[1]
    outs = send_ref.shape[1] // 4
    place, me = lax.axis_index("tp"), lax.axis_index("tok")
    other = pl.multiple_of((1 - me % 2) * outs, outs)
    total = early_ref[...]
    for o in (1, 3):
        at = pl.multiple_of((place ^ o) * outs_tp, outs_tp)
        total = total + lax.dot_general(
            cots[o][...], w_ref[:, pl.ds(at, outs_tp)], NT, preferred_element_type=F32
        )
    counts = jnp.zeros((pool_rows, 1), F32)
    maps = lax.rem(map_ref[...], jnp.int32(pool_rows))
    for n in range(maps.shape[0]):
        ids = lax.broadcasted_iota(jnp.int32, (pool_rows, maps.shape[1]), 0)
        hits = (maps[n : n + 1] == ids).astype(F32)
        counts = counts + jnp.sum(hits, axis=1, keepdims=True)
    turned = (total / counts).T.astype(BF16)
    for g in range(owners):
        turned_ref[g] = turned[g * feats : (g + 1) * feats]
    for o in range(4):
        for core in range(2):
            g = (me // 2 ^ o) * 2 + core
            outs_ref[o][core, :feats, :] = turned_ref[g]
            outs_ref[o][core, feats:, :] = pooled_ref[g]
    for o in range(4):
        send_ref[:, o * outs : (o + 1) * outs] = cots[o][:, pl.ds(other, outs)]


def project_kernel(w_ref, *refs):
    pieces, (kept_ref, passed_ref, sent_ref, pool_ref) = refs[:8], refs[8:]
    feats = pieces[0].shape[1] // 2
    outs_tp = kept_ref.shape[1]
    place = lax.axis_index("tp")
    targets = [kept_ref, sent_ref.at[0], passed_ref, sent_ref.at[1]]
    for g, piece, at in sources(pieces):
        pool_ref[g] = piece[at, feats:, :]
    pooled = jnp.concatenate([pool_ref[g] for g in range(len(pieces))], axis=0).T
    for o in (3, 1, 2, 0):
        at = pl.multiple_of((place ^ o) * outs_tp, outs_tp)
        targets[o][...] = lax.dot_general(
            pooled, w_ref[:, pl.ds(at, outs_tp)], NN, preferred_element_type=F32
        ).astype(BF16)


def gradient_kernel(came_ref, *refs):
    cots, pieces, (held_ref, gone_ref, part_ref, pool_ref) = refs[:4], refs[4:12], refs[12:]
    feats, pool_rows = pieces[0].shape[1] // 2, pieces[0].shape[2]
    outs = came_ref.shape[1] // 4
    place, me = lax.axis_index("tp"), lax.axis_index("tok")
    mine = pl.multiple_of((me % 2) * outs, outs)
    for g, piece, at in sources(pieces):
        pool_ref[g, :, :pool_rows] = piece[at, feats:, :]
        pool_ref[g, :, pool_rows:] = piece[1 - at, feats:, :]
    turned = jnp.concatenate([pool_ref[g] for g in range(len(pieces))], axis=0)
    for o in range(4):
        own = cots[o][:, pl.ds(mine, outs)]
        cot = jnp.concatenate([own, came_ref[:, o * outs : (o + 1) * outs]], axis=0)
        part_ref[place ^ o] = lax.dot_general(
            turned, cot, NN, preferred_element_type=F32
        ).astype(BF16)
    for o in range(4):
        (gone_ref if o % 2 else held_ref)[o // 2] = part_ref[(me // 2) ^ o]


def fold_shares_kernel(kept_ref, got_ref, share_ref):
    share_ref[...] = (kept_ref[...].astype(F32) + got_ref[1].astype(F32)).astype(BF16)


def fold_parts_kernel(held_ref, came_ref, part_ref):
    part_ref[...] = (held_ref[1].astype(F32) + came_ref[1].astype(F32)).astype(BF16)


def arrive_kernel(kept_ref, got_ref, share_ref, part_ref, projected_ref, part_out):
    total = kept_ref[...].astype(F32) + got_ref[0].astype(F32) + share_ref[...].astype(F32)
    projected_ref[...] = total.astype(BF16)
    part_out[...] = part_ref[...]


def finish_kernel(scale, *refs):
    pieces, (projected_ref, held_ref, came_ref, part_ref) = refs[:6], refs[6:10]
    tokens_out, projected_out, grad_out, all_ref, tokens_ref, grad_ref, sems = refs[10:]
    blocks, feats, rows = pieces[0].shape[0] // 2, *pieces[0].shape[1:]
    copies = []

    def send(source, target):
        copies.append(pltpu.make_async_copy(source, target, sems.at[len(copies)]))
        copies[-1].start()

    send(projected_ref, projected_out)
    total = held_ref[0].astype(F32) + came_ref[0].astype(F32) + part_ref[...].astype(F32)
    grad_ref[...] = total.T * scale
    send(grad_ref, grad_out)
    for g, piece, at in sources(pieces):
        lanes = pl.ds(pl.multiple_of(g * feats, feats), feats)
        all_ref[:, lanes, :] = piece[pl.ds(at * blocks, blocks)]
    for n in range(blocks):
        tokens_ref[n] = all_ref[n].T
        send(tokens_ref.at[n], tokens_out.at[n])
    for copy in copies:
        copy.wait()


def call(kernel, operands, out_shape, scratch, name, cost=0, out_space=pltpu.VMEM, in_space=pltpu.VMEM):
    several = isinstance(out_shape, (list, tuple))
    into = pl.BlockSpec(memory_space=in_space)
    if in_space == pltpu.HBM:
        operands = [pltpu.with_memory_space_constraint(a, pltpu.HBM) for a in operands]
    spaces = out_space if isinstance(out_space, tuple) else (out_space,) * (len(out_shape) if several else 1)
    out = [pl.BlockSpec(memory_space=space) for space in spaces]
    return pl.pallas_call(
        kernel,
        out_shape=out_shape,
        in_specs=[into] * len(operands),
        out_specs=out if several else out[0],
        scratch_shapes=scratch,
        compiler_params=pltpu.CompilerParams(vmem_limit_bytes=VMEM_LIMIT),
        cost_estimate=pl.CostEstimate(flops=cost, bytes_accessed=0, transcendentals=0),
        name=name,
    )(*operands)


def struct(*shape, dtype=BF16):
    return jax.ShapeDtypeStruct(shape, dtype)


def in_hbm(*shape, dtype=BF16):
    return pltpu.HBM(shape, dtype)


def swap(piece, axis, offset):
    size = lax.axis_size(axis)
    return lax.ppermute(piece, axis, [(i, i ^ offset) for i in range(size)])


def exchange(pieces, halves=False):
    came = [pieces[0]] + [swap(pieces[o], "tok", 2 * o) for o in (1, 2, 3)]
    if not halves:
        return came + [swap(piece, "tok", 1) for piece in came]
    count, *rest = pieces[0].shape
    others = call(gather_kernel, came[:3], struct(3, count // 2, *rest), [], "gather")
    return came + [swap(others, "tok", 1), swap(came[3], "tok", 1)]


def shards(tokens, mix_weights, proj_weight, pool_map, out_cot):
    toks, feats_tp = tokens.shape
    section_count, rows = mix_weights.shape[0], mix_weights.shape[-1]
    owners, groups = lax.axis_size("tok"), lax.axis_size("tp")
    pool_rows, outs_tp = out_cot.shape
    outs = outs_tp * groups // owners
    feats = feats_tp // owners
    blocks = toks // rows
    if feats % 16 or outs % 128 or owners != 8 or groups != 4 or pool_rows > 256 or blocks > TAIL:
        return general_shards(tokens, mix_weights, proj_weight, pool_map, out_cot)
    all_bits = (owners * blocks).bit_length() - 1
    section_bits = [section_id % all_bits for section_id in range(section_count)]
    fields = [pltpu.VMEM((owners * blocks, feats, rows), BF16)] * 2

    across = swap(out_cot, "tp", 2)
    beside = swap(out_cot, "tp", 1)
    onward = call(relay_kernel, (across, beside), struct(pool_rows, outs_tp), [], "relay", RELAY)
    cots = [out_cot, beside, across, swap(onward, "tp", 1)]
    maps = pool_map.reshape(blocks, rows)
    height = blocks * feats + TAIL
    packed = call(
        functools.partial(pack_kernel, pool_rows),
        (tokens.reshape(blocks, rows, feats_tp), maps),
        [struct(2, height, rows)] * 4,
        [
            pltpu.VMEM((blocks, rows, feats_tp), BF16),
            pltpu.VMEM((blocks, rows), jnp.int32),
            pltpu.VMEM((owners, height, rows), BF16),
            pltpu.SemaphoreType.DMA((blocks + 1,)),
        ],
        "pack",
        in_space=pltpu.HBM,
    )
    packed = exchange(packed, True)
    pooled, map_rows = call(
        functools.partial(forward_kernel, section_bits, blocks),
        (mix_weights, *packed),
        [struct(owners, feats, pool_rows), struct(owners, TAIL, rows)],
        fields,
        "forward_mix",
    )
    pooled, later = lax.optimization_barrier((pooled, across))
    early = call(
        early_kernel,
        (proj_weight, out_cot, later),
        struct(pool_rows, feats_tp, dtype=F32),
        [],
        "early_cotangent",
    )
    *both, half = call(
        cotangent_kernel,
        (proj_weight, maps, pooled, early, *cots),
        [struct(2, 2 * feats, pool_rows)] * 4 + [struct(pool_rows, groups * outs)],
        [pltpu.VMEM((owners, feats, pool_rows), BF16)],
        "cotangent",
    )
    half = swap(half, "tok", 1)
    both = exchange(both)

    kept, passed, sent = call(
        project_kernel,
        (proj_weight, *both),
        [struct(pool_rows, outs_tp)] * 2 + [struct(2, pool_rows, outs_tp)],
        [pltpu.VMEM((owners, feats, pool_rows), BF16)],
        "project",
    )
    half, passed = lax.optimization_barrier((half, passed))
    held, gone = call(
        gradient_kernel,
        (half, *cots, *both),
        [struct(2, feats_tp, outs)] * 2,
        [
            pltpu.VMEM((4, feats_tp, outs), BF16),
            pltpu.VMEM((owners, feats, 2 * pool_rows), BF16),
        ],
        "projector_gradient",
    )
    sent, gone = swap(sent, "tp", 1), swap(gone, "tok", 2)
    share = call(
        fold_shares_kernel,
        (passed, sent),
        struct(pool_rows, outs_tp),
        [],
        "fold_shares",
        0,
    )
    part = call(
        fold_parts_kernel, (held, gone), struct(feats_tp, outs), [], "fold_parts", 0
    )
    share = swap(share, "tp", 2)
    part = swap(part, "tok", 4)
    projected, part = call(
        arrive_kernel,
        (kept, sent, share, part),
        [struct(pool_rows, outs_tp), struct(feats_tp, outs)],
        [],
        "arrive",
        SUMS,
    )

    grad = call(
        functools.partial(backward_kernel, section_bits, blocks),
        (mix_weights, map_rows, *both),
        [struct(2 * blocks, feats, rows)] * 4,
        fields + [pltpu.VMEM((owners, feats, pool_rows), BF16)],
        "backward_mix",
    )
    token_grad, projected, proj_grad = call(
        functools.partial(finish_kernel, 1.0 / math.sqrt(pool_rows * owners)),
        (*exchange(grad, True), projected, held, gone, part),
        [
            in_hbm(blocks, rows, feats_tp),
            in_hbm(pool_rows, outs_tp),
            in_hbm(outs, feats_tp, dtype=F32),
        ],
        [
            pltpu.VMEM((blocks, feats_tp, rows), BF16),
            pltpu.VMEM((blocks, rows, feats_tp), BF16),
            pltpu.VMEM((outs, feats_tp), F32),
            pltpu.SemaphoreType.DMA((blocks + 2,)),
        ],
        "finish",
        out_space=pltpu.HBM,
    )
    token_grad = token_grad.reshape(toks, feats_tp)
    return (projected, token_grad, proj_grad)


def solution(mesh):
    in_specs = (P("tok", "tp"), P(), P("tp", None), P("tok"), P("tok", "tp"))
    out_specs = (P("tok", "tp"), P("tok", "tp"), P("tok", "tp"))
    return jax.shard_map(shards, mesh=mesh, in_specs=in_specs, out_specs=out_specs, check_vma=False)
```
